128 devices in a mesh: dp: 16 (over x, z_hi, core), ctx: 8 (over z_lo, y).
Axes of the slice: x: 4, y: 4, z: 4 (z_hi: 2, z_lo: 2; z = z_hi * 2 + z_lo), core: 2. Of those that a mesh axis runs over, the one named last changes fastest.
Arguments:
- normed: bfloat16 [16, 4096, 768], P('dp', 'ctx'), may hold values from -16 to 16
- cotangent: bfloat16 [16, 4096, 768], P('dp', 'ctx'), may hold values from -6 to 6
- qkv_weight: bfloat16 [768, 2304], replicated, may hold values from -0.375 to 0.375
- out_weight: bfloat16 [768, 768], replicated, may hold values from -0.21875 to 0.21875
Outputs:
- attention_out: bfloat16 [16, 4096, 768], P('dp', 'ctx')
- normed_grad: bfloat16 [16, 4096, 768], P('dp', 'ctx')
- qkv_grad: float32 [768, 2304], P('dp')
- out_grad: float32 [768, 768], P('dp')
The draws below stay inside these ranges and needn't reach their ends.
All inputs are finite; a program needn't handle non-finite values.
Results may differ from the reference program's by a relative error of at most 0.025.
Values may be sent and summed in bfloat16 or wider, within the bound.
No kernel may reach another device: no remote copies, remote signals or barrier semaphores. Data moves between devices by JAX's collectives and lax.ppermute only.
A program may use at most 128 MiB of HBM per device.

```python
import jax
import jax.numpy as jnp
from jax import lax

D = 768
HEADS = 12
HEAD_DIM = 64
ROW_LEN = 512
HALF = 6
ROWS = 8
SEQ = 4096
B = 16


def draw_normed(key, part):
    key = jax.random.fold_in(key, 11)
    first = jax.random.fold_in(key, 0)
    values = jax.random.truncated_normal(first, -4.0, 4.0, (B, SEQ, D), jnp.float32)
    return values.astype(jnp.bfloat16)


def draw_qkv_weight(key, part):
    key = jax.random.fold_in(key, 23)
    first = jax.random.fold_in(key, 0)
    factor = D ** (-0.5)
    values = jax.random.truncated_normal(first, -4.0, 4.0, (D, 3 * D), jnp.float32) * factor
    values = jnp.clip(values, -0.375, 0.375)
    return values.astype(jnp.bfloat16)


def strengthened(entries, key, source, target, shards_of, factor):
    def block_of(position):
        return (jnp.arange(entries.shape[position]) // (entries.shape[position] // shards_of)).reshape((-1,) + (1,) * (entries.ndim - 1 - position))

    first = jax.random.permutation(key, shards_of)[block_of(target)]
    far = (block_of(target) + shards_of // 2) % shards_of
    return jnp.where((block_of(source) == first) | (block_of(source) == far), factor * entries, entries)


def block_scale(key, extent, cuts, least, largest):
    factor_of, own = 1.0, jax.random.fold_in(key, 6)
    for position, parts in cuts:
        draws = jnp.exp(jax.random.uniform(jax.random.fold_in(own, position), (parts,), jnp.float32, least / len(cuts), largest / len(cuts)))
        factor_of = factor_of * jnp.repeat(draws, extent[position] // parts).reshape([-1 if axis == position else 1 for axis in range(len(extent))])
    return factor_of


def normal_values(rng, extent, scale, reach, shards=(), held_as=jnp.bfloat16):
    array = jax.random.normal(rng, extent, jnp.float32) * scale
    if len(shards) > 0:
        array = block_scale(rng, extent, shards, -0.22, 0.18) * array
    return jnp.clip(array, min=-reach, max=reach).astype(held_as)


def gaussian_with(stream_key, dims, scale, bound, shards, heavy, kind=jnp.bfloat16):
    entries = scale * jax.random.normal(stream_key, dims, jnp.float32)
    if shards:
        entries = entries * block_scale(stream_key, dims, shards, -0.22, 0.18)
    return jnp.clip(strengthened(entries, jax.random.fold_in(stream_key, 3), *heavy), -bound, bound).astype(kind)


def setup_inputs(seed: int = 0) -> dict:
    key_of = jax.random.split(jax.random.key(seed), 5)
    normed = draw_normed(jax.random.fold_in(key_of[4], 71), 0)
    cotangent = gaussian_with(key_of[1], (B, SEQ, D), 1.0, 6.0, ((0, 16), (1, 8)), (0, 2, 16, 2.0))
    qkv_weight = draw_qkv_weight(jax.random.fold_in(key_of[4], 71), 0)
    out_weight = normal_values(key_of[3], (D, D), D ** -0.5, 0.21875)
    return dict(normed=normed, cotangent=cotangent, qkv_weight=qkv_weight, out_weight=out_weight)


def attend(queries, key_part, value_part, grad_part):
    score_scale = queries.shape[-1] ** -0.5
    query_wide = queries.astype(jnp.float32)
    key_wide = key_part.astype(jnp.float32)
    value_wide = value_part.astype(jnp.float32)
    grad_wide = grad_part.astype(jnp.float32)
    scores = jnp.einsum("gihd,gjhd->ghij", query_wide, key_wide) * score_scale
    length = queries.shape[1]
    causal = lax.broadcasted_iota(jnp.int32, (length, length), 1) <= lax.broadcasted_iota(jnp.int32, (length, length), 0)
    scores = jnp.where(causal, scores, -1e30)
    top = jnp.max(scores, axis=-1, keepdims=True)
    weights = jnp.exp(scores - top)
    weights = weights / jnp.sum(weights, axis=-1, keepdims=True)
    rounded = weights.astype(jnp.bfloat16)
    rounded_wide = rounded.astype(jnp.float32)
    outputs = jnp.einsum("ghij,gjhd->gihd", rounded_wide, value_wide).astype(jnp.bfloat16)
    grad_weights = jnp.einsum("gihd,gjhd->ghij", grad_wide, value_wide)
    row_delta = jnp.sum(weights * grad_weights, axis=-1, keepdims=True)
    grad_scores = (weights * (grad_weights - row_delta) * score_scale).astype(jnp.bfloat16).astype(jnp.float32)
    grad_queries = jnp.einsum("ghij,gjhd->gihd", grad_scores, key_wide).astype(jnp.bfloat16)
    grad_keys = jnp.einsum("ghij,gihd->gjhd", grad_scores, query_wide).astype(jnp.bfloat16)
    grad_values = jnp.einsum("ghij,gihd->gjhd", rounded_wide, grad_wide).astype(jnp.bfloat16)
    return outputs, grad_queries, grad_keys, grad_values


def split_heads(block):
    shaped = block.reshape(ROWS, ROW_LEN, HEADS, HEAD_DIM)
    return shaped[:, :, :HALF], jnp.transpose(shaped[:, :, HALF:], (1, 0, 2, 3))


def join_heads(row_part, column_part):
    column_back = jnp.transpose(column_part, (1, 0, 2, 3))
    return jnp.concatenate([row_part, column_back], axis=2).reshape(SEQ, D)


def one_sequence(normed_seq, grad_seq, qkv_weight, out_weight):
    projected = jnp.dot(normed_seq, qkv_weight, preferred_element_type=jnp.float32).astype(jnp.bfloat16)
    grad_context = jnp.dot(grad_seq, out_weight, preferred_element_type=jnp.float32).astype(jnp.bfloat16)
    query_row, query_col = split_heads(projected[:, :D])
    key_row, key_col = split_heads(projected[:, D:2 * D])
    value_row, value_col = split_heads(projected[:, 2 * D:])
    grad_row, grad_col = split_heads(grad_context)
    row_results = attend(query_row, key_row, value_row, grad_row)
    col_results = attend(query_col, key_col, value_col, grad_col)
    joined = [join_heads(row_results[index], col_results[index]) for index in range(4)]
    context = joined[0]
    grad_projected = jnp.concatenate([joined[1], joined[2], joined[3]], axis=1)
    attention_out = jnp.dot(context, out_weight.T, preferred_element_type=jnp.float32).astype(jnp.bfloat16)
    normed_grad = jnp.dot(grad_projected, qkv_weight.T, preferred_element_type=jnp.float32).astype(jnp.bfloat16)
    qkv_term = jnp.dot(normed_seq.T, grad_projected, preferred_element_type=jnp.float32)
    out_term = jnp.dot(grad_seq.T, context, preferred_element_type=jnp.float32)
    return attention_out, normed_grad, qkv_term, out_term


def reference(normed, cotangent, qkv_weight, out_weight):
    def step(carry, pieces):
        attention_out, normed_grad, qkv_term, out_term = one_sequence(pieces[0], pieces[1], qkv_weight, out_weight)
        return (carry[0] + qkv_term, carry[1] + out_term), (attention_out, normed_grad)

    start = (jnp.zeros((D, 3 * D), jnp.float32), jnp.zeros((D, D), jnp.float32))
    totals, results = lax.scan(step, start, (normed, cotangent))
    factor = (B * SEQ) ** -0.5
    return results[0], results[1], totals[0] * factor, totals[1] * factor
```

```python
import functools

import jax
import jax.numpy as jnp
from jax import lax
from jax.experimental import pallas as pl
from jax.experimental.pallas import tpu as pltpu
from jax.sharding import PartitionSpec as P

WIDTH = 768
HALF_WIDTH = 384
HEAD_DIM = 64
POSITIONS = 512
ROWS = 8
COLUMNS = 64
PAIR = 128
PAIRS = HALF_WIDTH // PAIR
BLOCK = 256
CHUNK = 16
BF = jnp.bfloat16
F32 = jnp.float32
VMEM_LIMIT = 48 * 1024 * 1024


def dot(a, b):
    return lax.dot_general(a, b, (((1,), (0,)), ((), ())), preferred_element_type=F32)


def dot_nt(a, b):
    return lax.dot_general(a, b, (((1,), (1,)), ((), ())), preferred_element_type=F32)


def dot_tn(a, b):
    return lax.dot_general(a, b, (((0,), (0,)), ((), ())), preferred_element_type=F32)


def half_lanes(array, half):
    lane = lax.broadcasted_iota(jnp.int32, array.shape, array.ndim - 1)
    inside = (lane >= HEAD_DIM) if half else (lane < HEAD_DIM)
    return jnp.where(inside, array, jnp.zeros_like(array))


def probabilities(scores, allowed):
    scores = jnp.where(allowed, scores, -1e30)
    top = jnp.max(scores, axis=-1, keepdims=True)
    weights = jnp.exp(scores - top)
    return weights * (1.0 / jnp.sum(weights, axis=-1, keepdims=True))


def project(x_ref, c_ref, qkv_ref, out_ref, proj, gctx, first):
    x = x_ref[...].reshape(POSITIONS, WIDTH)
    for part in range(3):
        start = part * WIDTH + first
        piece = dot(x, qkv_ref[:, start : start + HALF_WIDTH]).astype(BF)
        if part == 0:
            piece = piece * BF(HEAD_DIM ** -0.5)
        proj[:, part * HALF_WIDTH : (part + 1) * HALF_WIDTH] = piece
    c = c_ref[...].reshape(POSITIONS, WIDTH)
    gctx[...] = dot(c, out_ref[:, first : first + HALF_WIDTH]).astype(BF)


def weight_terms(x_ref, c_ref, grads, ctx, terms, keep_ref, send_ref, core_ref, sems):
    x_t = jnp.transpose(x_ref[...].reshape(POSITIONS, WIDTH))
    for part in range(3):
        res = dot(x_t, grads[:, part * HALF_WIDTH : (part + 1) * HALF_WIDTH]).astype(BF)
        terms[:, :, part] = res.reshape(ROWS, 2, 48, HALF_WIDTH)
    c_t = jnp.transpose(c_ref[...].reshape(POSITIONS, WIDTH))
    terms[:, :, 3] = dot(c_t, ctx[...]).astype(BF).reshape(ROWS, 2, 48, HALF_WIDTH)
    core = core_ref[0]
    keep = pltpu.make_async_copy(terms.at[:, core], keep_ref, sems.at[0])
    send = pltpu.make_async_copy(terms.at[:, 1 - core], send_ref, sems.at[1])
    send.start()
    keep.start()
    send.wait()
    keep.wait()


def row_kernel(
    core_ref, x_ref, c_ref, qkv_ref, out_ref, grads, ctx, keep_ref, send_ref, proj, gctx, probs, dscores, terms, sems
):
    project(x_ref, c_ref, qkv_ref, out_ref, proj, gctx, 0)
    for pair in range(PAIRS):
        lanes = slice(pair * PAIR, (pair + 1) * PAIR)
        k_lanes = slice(HALF_WIDTH + pair * PAIR, HALF_WIDTH + (pair + 1) * PAIR)
        v_lanes = slice(2 * HALF_WIDTH + pair * PAIR, 2 * HALF_WIDTH + (pair + 1) * PAIR)
        keys = [half_lanes(proj[:, k_lanes], half) for half in range(2)]
        values = [half_lanes(proj[:, v_lanes], half) for half in range(2)]
        for start in range(0, POSITIONS, BLOCK):
            stop = start + BLOCK
            query = proj[start:stop, lanes]
            grad = gctx[start:stop, lanes]
            allowed = lax.broadcasted_iota(jnp.int32, (BLOCK, stop), 1) <= (
                lax.broadcasted_iota(jnp.int32, (BLOCK, stop), 0) + start
            )
            outs, dqs = [], []
            for half in range(2):
                key, value = keys[half][:stop], values[half][:stop]
                weights = probabilities(dot_nt(query, key), allowed)
                rounded = weights.astype(BF)
                probs[half, start:stop, :stop] = rounded
                outs.append(dot(rounded, value))
                grad_weights = dot_nt(grad, value)
                delta = jnp.sum(weights * grad_weights, axis=-1, keepdims=True)
                ds = (weights * (grad_weights - delta)).astype(BF)
                dscores[half, start:stop, :stop] = ds
                dqs.append(dot(ds, key))
            ctx[start:stop, lanes] = (outs[0] + outs[1]).astype(BF)
            grads[start:stop, lanes] = ((dqs[0] + dqs[1]) * (HEAD_DIM ** -0.5)).astype(BF)
        queries = [half_lanes(proj[:, lanes], half) for half in range(2)]
        grad_parts = [half_lanes(gctx[:, lanes], half) for half in range(2)]
        for start in range(0, POSITIONS, BLOCK):
            stop = start + BLOCK
            dk = sum(dot_tn(dscores[half, start:, start:stop], queries[half][start:]) for half in range(2))
            dv = sum(dot_tn(probs[half, start:, start:stop], grad_parts[half][start:]) for half in range(2))
            grads[start:stop, k_lanes] = dk.astype(BF)
            grads[start:stop, v_lanes] = dv.astype(BF)
    weight_terms(x_ref, c_ref, grads, ctx, terms, keep_ref, send_ref, core_ref, sems)


def column_kernel(
    core_ref, x_ref, c_ref, qkv_ref, out_ref, grads, ctx, keep_ref, send_ref, proj, gctx, terms, sems
):
    project(x_ref, c_ref, qkv_ref, out_ref, proj, gctx, HALF_WIDTH)
    size = ROWS * CHUNK
    chunks = COLUMNS // CHUNK
    line = lax.broadcasted_iota(jnp.int32, (size, size), 0)
    across = lax.broadcasted_iota(jnp.int32, (size, size), 1)
    allowed = ((line % CHUNK) == (across % CHUNK)) & (across <= line)
    allowed = jnp.concatenate([allowed.astype(F32)] * chunks, axis=0) > 0

    def gather(ref, base):
        whole = ref[:, base : base + PAIR].reshape(ROWS, COLUMNS, PAIR)
        return [
            whole[:, t * CHUNK : (t + 1) * CHUNK].reshape(size, PAIR) for t in range(chunks)
        ]

    def scatter(ref, base, pieces):
        whole = jnp.concatenate([p.reshape(ROWS, CHUNK, PAIR) for p in pieces], axis=1)
        ref[:, base : base + PAIR] = whole.reshape(POSITIONS, PAIR)

    for pair in range(PAIRS):
        base = pair * PAIR
        query, key, value = [gather(proj, part * HALF_WIDTH + base) for part in range(3)]
        grad = gather(gctx, base)
        outs, dqs, dks, dvs = [], [], [], []
        for half in range(2):
            key_h = [half_lanes(t, half) for t in key]
            value_h = [half_lanes(t, half) for t in value]
            query_h = [half_lanes(t, half) for t in query]
            grad_h = [half_lanes(t, half) for t in grad]
            scores = jnp.concatenate([dot_nt(a, b) for a, b in zip(query, key_h)], axis=0)
            grad_weights = jnp.concatenate([dot_nt(a, b) for a, b in zip(grad, value_h)], axis=0)
            weights = probabilities(scores, allowed)
            rounded = weights.astype(BF)
            delta = jnp.sum(weights * grad_weights, axis=-1, keepdims=True)
            ds = (weights * (grad_weights - delta)).astype(BF)
            rounded = [rounded[t * size : (t + 1) * size] for t in range(chunks)]
            ds = [ds[t * size : (t + 1) * size] for t in range(chunks)]
            outs.append([dot(a, b) for a, b in zip(rounded, value_h)])
            dqs.append([dot(a, b) for a, b in zip(ds, key_h)])
            dks.append([dot_tn(a, b) for a, b in zip(ds, query_h)])
            dvs.append([dot_tn(a, b) for a, b in zip(rounded, grad_h)])
        scatter(ctx, base, [(a + b).astype(BF) for a, b in zip(*outs)])
        scatter(grads, base, [((a + b) * (HEAD_DIM ** -0.5)).astype(BF) for a, b in zip(*dqs)])
        scatter(grads, HALF_WIDTH + base, [(a + b).astype(BF) for a, b in zip(*dks)])
        scatter(grads, 2 * HALF_WIDTH + base, [(a + b).astype(BF) for a, b in zip(*dvs)])
    weight_terms(x_ref, c_ref, grads, ctx, terms, keep_ref, send_ref, core_ref, sems)


def return_kernel(grads, ctx, qkv_ref, back_ref):
    total = sum(
        dot_nt(
            grads[:, part * HALF_WIDTH : (part + 1) * HALF_WIDTH],
            qkv_ref[:, part * WIDTH + HALF_WIDTH : (part + 1) * WIDTH],
        )
        for part in range(3)
    )
    back_ref[:, :WIDTH] = total.astype(BF)
    back_ref[:, WIDTH:] = ctx[...]


def final_kernel(grads, ctx, back_ref, qkv_ref, out_ref, attention_ref, normed_ref):
    total = back_ref[:, :WIDTH].astype(F32)
    for part in range(3):
        total += dot_nt(
            grads[:, part * HALF_WIDTH : (part + 1) * HALF_WIDTH],
            qkv_ref[:, part * WIDTH : part * WIDTH + HALF_WIDTH],
        )
    normed_ref[...] = total.astype(BF)
    attention_ref[...] = (
        dot_nt(ctx[...], out_ref[:, :HALF_WIDTH]) + dot_nt(back_ref[:, WIDTH:], out_ref[:, HALF_WIDTH:])
    ).astype(BF)


VMEM = pl.BlockSpec(memory_space=pltpu.VMEM)


def cost(flops, transcendentals=0):
    return pl.CostEstimate(flops=flops, bytes_accessed=8 * 2 ** 20, transcendentals=transcendentals)


def sublayer(kernel, scratch, core, x, c, qkv_weight, out_weight):
    return pl.pallas_call(
        kernel,
        out_shape=(
            jax.ShapeDtypeStruct((POSITIONS, 3 * HALF_WIDTH), BF),
            jax.ShapeDtypeStruct((POSITIONS, HALF_WIDTH), BF),
            jax.ShapeDtypeStruct((ROWS, 4, 48, HALF_WIDTH), BF),
            jax.ShapeDtypeStruct((ROWS, 4, 48, HALF_WIDTH), BF),
        ),
        in_specs=[pl.BlockSpec(memory_space=pltpu.SMEM)] + [VMEM] * 4,
        out_specs=(VMEM, VMEM, pl.BlockSpec(memory_space=pl.ANY), pl.BlockSpec(memory_space=pl.ANY)),
        scratch_shapes=[
            pltpu.VMEM((POSITIONS, 3 * HALF_WIDTH), BF),
            pltpu.VMEM((POSITIONS, HALF_WIDTH), BF),
            *scratch,
            pltpu.VMEM((ROWS, 2, 4, 48, HALF_WIDTH), BF),
            pltpu.SemaphoreType.DMA((2,)),
        ],
        compiler_params=pltpu.CompilerParams(vmem_limit_bytes=VMEM_LIMIT),
        cost_estimate=cost(4 * 10 ** 9),
    )(core, x, c, qkv_weight, out_weight)


def swap(part, axis, groups=None):
    return lax.all_to_all(part, axis, split_axis=0, concat_axis=0, tiled=True, axis_index_groups=groups)


def other_groups():
    def flat(x, z_hi, core, z_lo, y):
        return ((x * 2 + z_hi) * 2 + core) * 8 + z_lo * 4 + y

    return [
        [flat(x, z_hi, core, z_lo, y) for x in range(4) for z_hi in range(2) for y in range(4) for z_lo in range(2)]
        for core in range(2)
    ]


def summed(keep, send):
    received = lax.ppermute(send, "dp", [(i, i ^ 1) for i in range(16)])
    both = (keep.astype(F32) + received.astype(F32)).astype(BF)
    pieces = swap(both.reshape(64, 24, HALF_WIDTH), ("dp", "ctx"), other_groups())
    return jnp.sum(pieces.astype(F32), axis=0).astype(BF)


def body(normed, cotangent, qkv_weight, out_weight):
    x, c = normed[0], cotangent[0]
    core = (lax.axis_index("dp") % 2).reshape(1)
    both = jnp.concatenate([x, c], axis=1).reshape(ROWS, COLUMNS, 2 * WIDTH)
    moved = swap(both, "ctx").reshape(POSITIONS, 2 * WIDTH)
    x_col, c_col = moved[:, :WIDTH], moved[:, WIDTH:]
    grads_row, ctx_row, keep_row, send_row = sublayer(
        row_kernel,
        [pltpu.VMEM((2, POSITIONS, POSITIONS), BF)] * 2,
        core, x, c, qkv_weight, out_weight,
    )
    sum_row = summed(keep_row, send_row)
    grads_col, ctx_col, keep_col, send_col = sublayer(
        column_kernel, [], core, x_col, c_col, qkv_weight, out_weight
    )
    sum_col = summed(keep_col, send_col)
    back = pl.pallas_call(
        return_kernel,
        out_shape=jax.ShapeDtypeStruct((POSITIONS, WIDTH + HALF_WIDTH), BF),
        in_specs=[VMEM] * 3,
        out_specs=VMEM,
        compiler_params=pltpu.CompilerParams(vmem_limit_bytes=VMEM_LIMIT),
        cost_estimate=cost(10 ** 9),
    )(grads_col, ctx_col, qkv_weight)
    back = swap(back.reshape(ROWS, COLUMNS, WIDTH + HALF_WIDTH), "ctx").reshape(POSITIONS, WIDTH + HALF_WIDTH)
    attention_out, normed_grad = pl.pallas_call(
        final_kernel,
        out_shape=(jax.ShapeDtypeStruct((POSITIONS, WIDTH), BF),) * 2,
        in_specs=[VMEM] * 5,
        out_specs=(VMEM, VMEM),
        compiler_params=pltpu.CompilerParams(vmem_limit_bytes=VMEM_LIMIT),
        cost_estimate=cost(2 * 10 ** 9),
    )(grads_row, ctx_row, back, qkv_weight, out_weight)
    own = jnp.stack([sum_row, sum_col])
    whole = swap(jnp.broadcast_to(own[None], (8,) + own.shape), "ctx")
    factor = (lax.axis_size("dp") * lax.axis_size("ctx") * POSITIONS) ** (-0.5)
    whole = whole.reshape(2, 4, 2, 24, HALF_WIDTH).astype(F32) * factor
    whole = jnp.transpose(whole, (0, 3, 1, 2, 4)).reshape(48, 8 * HALF_WIDTH)
    return (attention_out[None], normed_grad[None], whole[:, : 3 * WIDTH], whole[:, 3 * WIDTH :])


def solution(mesh):
    placed = (P("dp", "ctx", None), P("dp", "ctx", None), P(), P())
    return jax.shard_map(
        body,
        mesh=mesh,
        in_specs=placed,
        out_specs=(P("dp", "ctx", None), P("dp", "ctx", None), P("dp", None), P("dp", None)),
        check_vma=False,
    )
```

```python
import functools

import jax
import jax.numpy as jnp
from jax import lax
from jax.experimental import pallas as pl
from jax.experimental.pallas import tpu as pltpu
from jax.sharding import PartitionSpec as P

WIDTH = 768
HALF_WIDTH = 384
HEAD_DIM = 64
POSITIONS = 512
ROWS = 8
COLUMNS = 64
PAIR = 128
PAIRS = HALF_WIDTH // PAIR
BLOCK = 256
CHUNK = 16
BF = jnp.bfloat16
F32 = jnp.float32
MIB = 1024 * 1024


def dot(a, b):
    return lax.dot_general(a, b, (((1,), (0,)), ((), ())), preferred_element_type=F32)


def dot_nt(a, b):
    return lax.dot_general(a, b, (((1,), (1,)), ((), ())), preferred_element_type=F32)


def dot_tn(a, b):
    return lax.dot_general(a, b, (((0,), (0,)), ((), ())), preferred_element_type=F32)


def half_lanes(array, half):
    lane = lax.broadcasted_iota(jnp.int32, array.shape, array.ndim - 1)
    inside = (lane >= HEAD_DIM) if half else (lane < HEAD_DIM)
    return jnp.where(inside, array, jnp.zeros_like(array))


def probabilities(scores, allowed):
    scores = jnp.where(allowed, scores, -1e30)
    top = jnp.max(scores, axis=-1, keepdims=True)
    weights = jnp.exp(scores - top)
    return weights * (1.0 / jnp.sum(weights, axis=-1, keepdims=True))


def load(x_hbm, c_hbm, qkv_hbm, out_hbm, x, c, w_qkv, w_out, sems, first):
    copies = [pltpu.make_async_copy(x_hbm, x, sems.at[0])]
    for part in range(3):
        columns = pl.ds(part * WIDTH + first, HALF_WIDTH)
        place = pl.ds(part * HALF_WIDTH, HALF_WIDTH)
        copies.append(pltpu.make_async_copy(qkv_hbm.at[:, columns], w_qkv.at[:, place], sems.at[1 + part]))
    copies.append(pltpu.make_async_copy(c_hbm, c, sems.at[4]))
    copies.append(pltpu.make_async_copy(out_hbm.at[:, pl.ds(first, HALF_WIDTH)], w_out, sems.at[5]))
    for copy in copies:
        copy.start()
    return copies


def project(copies, x, c, w_qkv, w_out, proj, gctx):
    for copy in copies[:4]:
        copy.wait()
    for part, piece in enumerate(jnp.split(dot(x[...].reshape(POSITIONS, WIDTH), w_qkv[...]), 3, axis=1)):
        piece = piece.astype(BF)
        if part == 0:
            piece = piece * BF(HEAD_DIM ** -0.5)
        proj[:, part * HALF_WIDTH : (part + 1) * HALF_WIDTH] = piece
    copies[4].wait()
    copies[5].wait()
    gctx[...] = dot(c[...].reshape(POSITIONS, WIDTH), w_out[...]).astype(BF)


def weight_terms(x, c, grads, ctx, terms, targets, sems, extra):
    copies = []
    for part in range(4):
        for index, (place, target) in enumerate(targets):
            copies.append(
                pltpu.make_async_copy(terms.at[:, place, part], target.at[:, part], sems.at[2 + 4 * index + part])
            )
    extra = start_all(
        [pltpu.make_async_copy(source, target, sems.at[index]) for index, (source, target) in enumerate(extra)]
    )
    x_t = jnp.transpose(x[...].reshape(POSITIONS, WIDTH))
    for part in range(3):
        res = dot(x_t, grads[:, part * HALF_WIDTH : (part + 1) * HALF_WIDTH]).astype(BF)
        terms[:, :, part] = res.reshape(ROWS, 2, 48, HALF_WIDTH)
        copies[2 * part].start()
        copies[2 * part + 1].start()
    c_t = jnp.transpose(c[...].reshape(POSITIONS, WIDTH))
    terms[:, :, 3] = dot(c_t, ctx[...]).astype(BF).reshape(ROWS, 2, 48, HALF_WIDTH)
    copies[6].start()
    copies[7].start()
    wait_all(extra + copies)


def row_kernel(
    core_ref, x_hbm, c_hbm, qkv_hbm, out_hbm, grads_hbm, ctx_hbm, keep_hbm, send_hbm,
    x, c, w_qkv, w_out, proj, gctx, grads, ctx, terms, sems, probs, dscores,
):
    copies = load(x_hbm, c_hbm, qkv_hbm, out_hbm, x, c, w_qkv, w_out, sems, 0)
    project(copies, x, c, w_qkv, w_out, proj, gctx)
    for pair in range(PAIRS):
        lanes = slice(pair * PAIR, (pair + 1) * PAIR)
        k_lanes = slice(HALF_WIDTH + pair * PAIR, HALF_WIDTH + (pair + 1) * PAIR)
        v_lanes = slice(2 * HALF_WIDTH + pair * PAIR, 2 * HALF_WIDTH + (pair + 1) * PAIR)
        keys = [half_lanes(proj[:, k_lanes], half) for half in range(2)]
        values = [half_lanes(proj[:, v_lanes], half) for half in range(2)]
        for start in range(0, POSITIONS, BLOCK):
            stop = start + BLOCK
            query = proj[start:stop, lanes]
            grad = gctx[start:stop, lanes]
            allowed = lax.broadcasted_iota(jnp.int32, (BLOCK, stop), 1) <= (
                lax.broadcasted_iota(jnp.int32, (BLOCK, stop), 0) + start
            )
            outs, dqs = [], []
            for half in range(2):
                key, value = keys[half][:stop], values[half][:stop]
                weights = probabilities(dot_nt(query, key), allowed)
                rounded = weights.astype(BF)
                probs[half, start:stop, :stop] = rounded
                outs.append(dot(rounded, value))
                grad_weights = dot_nt(grad, value)
                delta = jnp.sum(weights * grad_weights, axis=-1, keepdims=True)
                ds = (weights * (grad_weights - delta)).astype(BF)
                dscores[half, start:stop, :stop] = ds
                dqs.append(dot(ds, key))
            ctx[start:stop, lanes] = (outs[0] + outs[1]).astype(BF)
            grads[start:stop, lanes] = ((dqs[0] + dqs[1]) * (HEAD_DIM ** -0.5)).astype(BF)
        queries = [half_lanes(proj[:, lanes], half) for half in range(2)]
        grad_parts = [half_lanes(gctx[:, lanes], half) for half in range(2)]
        for start in range(0, POSITIONS, BLOCK):
            stop = start + BLOCK
            dk = sum(dot_tn(dscores[half, start:, start:stop], queries[half][start:]) for half in range(2))
            dv = sum(dot_tn(probs[half, start:, start:stop], grad_parts[half][start:]) for half in range(2))
            grads[start:stop, k_lanes] = dk.astype(BF)
            grads[start:stop, v_lanes] = dv.astype(BF)
    core = core_ref[0]
    targets = [(1 - core, send_hbm), (core, keep_hbm)]
    weight_terms(x, c, grads, ctx, terms, targets, sems, [(grads, grads_hbm), (ctx, ctx_hbm)])


def column_kernel(
    core_ref, both_hbm, qkv_hbm, out_hbm, after, back_hbm, keep_hbm, send_hbm,
    x, c, w_qkv, w_out, proj, gctx, grads, ctx, terms, sems, back,
):
    x_hbm, c_hbm = both_hbm.at[:, 0], both_hbm.at[:, 1]
    copies = load(x_hbm, c_hbm, qkv_hbm, out_hbm, x, c, w_qkv, w_out, sems, HALF_WIDTH)
    project(copies, x, c, w_qkv, w_out, proj, gctx)
    size = ROWS * CHUNK
    chunks = COLUMNS // CHUNK
    line = lax.broadcasted_iota(jnp.int32, (size, size), 0)
    across = lax.broadcasted_iota(jnp.int32, (size, size), 1)
    allowed = ((line % CHUNK) == (across % CHUNK)) & (across <= line)
    allowed = jnp.concatenate([allowed.astype(F32)] * chunks, axis=0) > 0

    def twice(array):
        return jnp.concatenate([half_lanes(array, 0), half_lanes(array, 1)], axis=0)

    def gather(ref, base):
        whole = ref[:, base : base + PAIR].reshape(ROWS, COLUMNS, PAIR)
        return [
            whole[:, t * CHUNK : (t + 1) * CHUNK].reshape(size, PAIR) for t in range(chunks)
        ]

    def scatter(ref, base, pieces):
        whole = jnp.concatenate([p.reshape(ROWS, CHUNK, PAIR) for p in pieces], axis=1)
        ref[:, base : base + PAIR] = whole.reshape(POSITIONS, PAIR)

    for pair in range(PAIRS):
        base = pair * PAIR
        query, key, value = [gather(proj, part * HALF_WIDTH + base) for part in range(3)]
        grad = gather(gctx, base)
        keys, values, queries, grad_parts = [[twice(t) for t in part] for part in (key, value, query, grad)]
        scores = jnp.concatenate([dot_nt(a, b) for a, b in zip(query, keys)], axis=0)
        grad_weights = jnp.concatenate([dot_nt(a, b) for a, b in zip(grad, values)], axis=0)
        rounded, dscores = [], []
        for half in range(2):
            lanes = slice(half * size, (half + 1) * size)
            weights = probabilities(scores[:, lanes], allowed)
            rounded.append(weights.astype(BF))
            part = grad_weights[:, lanes]
            delta = jnp.sum(weights * part, axis=-1, keepdims=True)
            dscores.append((weights * (part - delta)).astype(BF))
        outs, dqs, dks, dvs = [], [], [], []
        for t in range(chunks):
            rows = slice(t * size, (t + 1) * size)
            wide = [jnp.concatenate([pieces[0][rows], pieces[1][rows]], axis=1) for pieces in (rounded, dscores)]
            tall = [jnp.concatenate([pieces[0][rows], pieces[1][rows]], axis=0) for pieces in (rounded, dscores)]
            outs.append(dot(wide[0], values[t]).astype(BF))
            dqs.append((dot(wide[1], keys[t]) * (HEAD_DIM ** -0.5)).astype(BF))
            dks.append(dot_tn(tall[1], queries[t]).astype(BF))
            dvs.append(dot_tn(tall[0], grad_parts[t]).astype(BF))
        scatter(ctx, base, outs)
        scatter(grads, base, dqs)
        scatter(grads, HALF_WIDTH + base, dks)
        scatter(grads, 2 * HALF_WIDTH + base, dvs)
    core = core_ref[0]
    targets = [(1 - core, send_hbm), (core, keep_hbm)]
    back[:, WIDTH:] = ctx[...]
    for start in range(0, WIDTH, BLOCK):
        columns = slice(start, start + BLOCK)
        back[:, columns] = dot_nt(grads[...], w_qkv[columns]).astype(BF)
    weight_terms(x, c, grads, ctx, terms, targets, sems, [(back, back_hbm)])


def wait_all(copies):
    for copy in copies:
        copy.wait()


def start_all(copies):
    for copy in copies:
        copy.start()
    return copies


def weight_copies(qkv_hbm, w_qkv, sems, first):
    return [
        pltpu.make_async_copy(
            qkv_hbm.at[:, pl.ds(part * WIDTH + first, HALF_WIDTH)], w_qkv.at[part], sems.at[part]
        )
        for part in range(3)
    ]


def grads_times_weights(grads, w_qkv, columns):
    return sum(
        dot_nt(grads[:, part * HALF_WIDTH : (part + 1) * HALF_WIDTH], w_qkv[part, columns]) for part in range(3)
    )


def final_kernel(
    grads_hbm, ctx_hbm, back_hbm, qkv_hbm, out_hbm, attention_hbm, normed_hbm,
    grads, ctx, back, w_qkv, w_out, attention, normed, sems, out_sems,
):
    ins = start_all(
        [
            pltpu.make_async_copy(source, target, sems.at[3 + index])
            for index, (source, target) in enumerate(
                ((ctx_hbm, ctx), (back_hbm, back), (out_hbm, w_out), (grads_hbm, grads))
            )
        ]
        + weight_copies(qkv_hbm, w_qkv, sems, 0)
    )
    outs = []
    wait_all(ins[:3])
    for index in range(3):
        columns = slice(index * BLOCK, (index + 1) * BLOCK)
        span = pl.ds(index * BLOCK, BLOCK)
        attention[:, columns] = (
            dot_nt(ctx[...], w_out[columns, :HALF_WIDTH]) + dot_nt(back[:, WIDTH:], w_out[columns, HALF_WIDTH:])
        ).astype(BF)
        outs += start_all(
            [pltpu.make_async_copy(attention.at[:, span], attention_hbm.at[:, span], out_sems.at[0, index])]
        )
    wait_all(ins[3:])
    for index in range(3):
        columns = slice(index * BLOCK, (index + 1) * BLOCK)
        span = pl.ds(index * BLOCK, BLOCK)
        normed[:, columns] = (
            back[:, columns].astype(F32) + grads_times_weights(grads, w_qkv, columns)
        ).astype(BF)
        outs += start_all([pltpu.make_async_copy(normed.at[:, span], normed_hbm.at[:, span], out_sems.at[1, index])])
    wait_all(outs)


def order_kernel(back_hbm, first, second, third, out_hbm, zeros, sems):
    zeros[...] = jnp.zeros_like(zeros)
    wait_all(start_all([pltpu.make_async_copy(zeros, out_hbm, sems.at[0])]))


def pack_kernel(x_hbm, c_hbm, both_hbm, both, sems, out_sems):
    spans = [pl.ds(2 * index, 2) for index in range(4)]
    ins = start_all(
        [
            pltpu.make_async_copy(source.at[span], both.at[span, place], sems.at[place, index])
            for index, span in enumerate(spans)
            for place, source in enumerate((x_hbm, c_hbm))
        ]
    )
    outs = []
    for index, span in enumerate(spans):
        wait_all(ins[2 * index : 2 * index + 2])
        outs += start_all([pltpu.make_async_copy(both.at[span], both_hbm.at[span], out_sems.at[index])])
    wait_all(outs)


def pair_sum_kernel(x_ref, keep_hbm, received_hbm, *refs):
    out_hbms = refs[-8:-4]
    terms, totals, sems, out_sems = refs[-4:]
    ins, outs = [], []
    order = (1, 3, 2, 0)
    for step in order:
        place = pl.ds(2 * lax.rem(x_ref[0] + step, 4), 2)
        for index, source in enumerate((keep_hbm, received_hbm)):
            ins += start_all(
                [pltpu.make_async_copy(source.at[place], terms.at[step, index], sems.at[index, step])]
            )
    for index, step in enumerate(order):
        wait_all(ins[2 * index : 2 * index + 2])
        totals[step] = (terms[step, 0].astype(F32) + terms[step, 1].astype(F32)).astype(BF)
        outs += start_all([pltpu.make_async_copy(totals.at[step], out_hbms[step], out_sems.at[step])])
    wait_all(outs)


def ring_sum_kernel(*refs):
    in_hbms, (out_hbm, terms, totals, sems, out_sems) = refs[:8], refs[9:]
    ins = start_all(
        [pltpu.make_async_copy(source, terms.at[index], sems.at[index]) for index, source in enumerate(in_hbms)]
    )
    outs = []
    for half in range(2):
        wait_all(ins[4 * half : 4 * half + 4])
        for z_hi in range(2):
            total = sum(terms[4 * half + step, z_hi].astype(F32) for step in range(4))
            for z_lo in range(2):
                totals[z_hi, :, z_lo, half] = total[:, 24 * z_lo : 24 * z_lo + 24].astype(BF)
    for z_hi in range(2):
        outs += start_all([pltpu.make_async_copy(totals.at[z_hi], out_hbm.at[z_hi], out_sems.at[z_hi])])
    wait_all(outs)


def group_sum_kernel(pieces_hbm, out_hbm, pieces, total, sems):
    wait_all(start_all([pltpu.make_async_copy(pieces_hbm, pieces, sems.at[8])]))
    total[...] = jnp.sum(pieces[...].astype(F32), axis=0).astype(BF)
    wait_all(
        start_all([pltpu.make_async_copy(total, out_hbm.at[place], sems.at[place]) for place in range(8)])
    )


def assemble_kernel(factor, whole_hbm, qkv_hbm, out_hbm, whole, qkv_grad, out_grad, sems):
    wait_all(start_all([pltpu.make_async_copy(whole_hbm, whole, sems.at[0])]))
    for place in range(8):
        rows = slice(place // 4 * 24, place // 4 * 24 + 24)
        part = place % 4
        for half in range(2):
            start = half * HALF_WIDTH
            value = whole[place, half].astype(F32) * factor
            if part < 3:
                start += part * WIDTH
                qkv_grad[rows, start : start + HALF_WIDTH] = value
            else:
                out_grad[rows, start : start + HALF_WIDTH] = value
    wait_all(
        start_all(
            [
                pltpu.make_async_copy(qkv_grad, qkv_hbm, sems.at[1]),
                pltpu.make_async_copy(out_grad, out_hbm, sems.at[2]),
            ]
        )
    )


SMEM = pl.BlockSpec(memory_space=pltpu.SMEM)
HBM = pl.BlockSpec(memory_space=pltpu.HBM)


def buffer(*dims, dtype=BF):
    return pltpu.VMEM(dims, dtype)


def copy_sems(*dims):
    return pltpu.SemaphoreType.DMA(dims)


def shape(*dims, dtype=BF):
    return jax.ShapeDtypeStruct(dims, dtype)


def call(kernel, out_shape, flops, scratch, arrays, mib=64):
    scalars = sum(1 for array in arrays if array.ndim == 1)
    return pl.pallas_call(
        kernel,
        out_shape=out_shape,
        in_specs=[SMEM] * scalars + [HBM] * (len(arrays) - scalars),
        out_specs=jax.tree.map(lambda _: HBM, out_shape),
        scratch_shapes=scratch,
        compiler_params=pltpu.CompilerParams(vmem_limit_bytes=mib * MIB),
        cost_estimate=pl.CostEstimate(flops=flops, bytes_accessed=2 ** 16, transcendentals=0),
    )(*arrays)


def sublayer(kernel, dims, out_shapes, scratch, *arrays):
    return call(
        kernel,
        (*out_shapes, shape(ROWS, 4, 48, HALF_WIDTH), shape(ROWS, 4, 48, HALF_WIDTH)),
        2 * 10 ** 10,
        [
            buffer(*dims),
            buffer(*dims),
            buffer(WIDTH, 3 * HALF_WIDTH),
            buffer(WIDTH, HALF_WIDTH),
            buffer(POSITIONS, 3 * HALF_WIDTH),
            buffer(POSITIONS, HALF_WIDTH),
            buffer(POSITIONS, 3 * HALF_WIDTH),
            buffer(POSITIONS, HALF_WIDTH),
            buffer(ROWS, 2, 4, 48, HALF_WIDTH),
            copy_sems(10),
            *scratch,
        ],
        arrays,
        mib=64,
    )


def swap(part, axis, groups=None):
    return lax.all_to_all(part, axis, split_axis=0, concat_axis=0, tiled=True, axis_index_groups=groups)


def plane_groups():
    def flat(x, z_hi, core, z_lo, y):
        return ((x * 2 + z_hi) * 2 + core) * 8 + z_lo * 4 + y

    return [
        [flat(x, z_hi, core, z_lo, y) for z_hi in range(2) for y in range(4) for z_lo in range(2)]
        for x in range(4)
        for core in range(2)
    ]


def exchange(send):
    return lax.ppermute(send, "dp", [(i, i ^ 1) for i in range(16)])


def pair_sum(x_index, keep, send, *after):
    return call(
        pair_sum_kernel,
        (shape(2, 4, 48, HALF_WIDTH),) * 4,
        2 * 10 ** 9,
        [buffer(4, 2, 2, 4, 48, HALF_WIDTH), buffer(4, 2, 4, 48, HALF_WIDTH), copy_sems(2, 4), copy_sems(4)],
        (x_index, keep, exchange(send), *after),
    )


def ring(parts):
    return [parts[0]] + [
        lax.ppermute(parts[step], "dp", [(i, (i + 4 * step) % 16) for i in range(16)]) for step in range(1, 4)
    ]


def body(normed, cotangent, qkv_weight, out_weight):
    x, c = normed[0], cotangent[0]
    dp = lax.axis_index("dp")
    core = (dp % 2).reshape(1)
    x_index = (dp // 4).reshape(1)
    grid_dims = (ROWS, COLUMNS, WIDTH)
    both = call(
        pack_kernel,
        shape(ROWS, 2, COLUMNS, WIDTH),
        10 ** 6,
        [buffer(ROWS, 2, COLUMNS, WIDTH), copy_sems(2, 4), copy_sems(4)],
        (x.reshape(grid_dims), c.reshape(grid_dims)),
    )
    both = swap(both, "ctx")
    grads_row, ctx_row, keep_row, send_row = sublayer(
        row_kernel,
        (POSITIONS, WIDTH),
        [shape(POSITIONS, 3 * HALF_WIDTH), shape(POSITIONS, HALF_WIDTH)],
        [buffer(2, POSITIONS, POSITIONS)] * 2,
        core, x, c, qkv_weight, out_weight,
    )
    terms_row = ring(pair_sum(x_index, keep_row, send_row))
    back_width = WIDTH + HALF_WIDTH
    back, keep_col, send_col = sublayer(
        column_kernel,
        grid_dims,
        [shape(POSITIONS, back_width)],
        [buffer(POSITIONS, back_width)],
        core, both, qkv_weight, out_weight, terms_row[0],
    )
    order = call(order_kernel, shape(8, PAIR, dtype=F32), 4 * 10 ** 10, [buffer(8, PAIR, dtype=F32), copy_sems(1)], (back, *terms_row[1:]))
    parts = pair_sum(x_index, keep_col, send_col, order)
    terms_col = ring(parts)
    back = swap(back.reshape(ROWS, COLUMNS, back_width), "ctx").reshape(POSITIONS, back_width)
    attention_out, normed_grad = call(
        final_kernel,
        (shape(POSITIONS, WIDTH),) * 2,
        4 * 10 ** 9,
        [
            buffer(POSITIONS, 3 * HALF_WIDTH),
            buffer(POSITIONS, HALF_WIDTH),
            buffer(POSITIONS, back_width),
            buffer(3, WIDTH, HALF_WIDTH),
            buffer(WIDTH, WIDTH),
            buffer(POSITIONS, WIDTH),
            buffer(POSITIONS, WIDTH),
            copy_sems(7),
            copy_sems(2, 4),
        ],
        (grads_row, ctx_row, back, qkv_weight, out_weight),
        mib=64,
    )
    terms = call(
        ring_sum_kernel,
        shape(2, 4, 2, 2, 24, HALF_WIDTH),
        2 * 10 ** 9,
        [buffer(8, 2, 4, 48, HALF_WIDTH), buffer(2, 4, 2, 2, 24, HALF_WIDTH), copy_sems(8), copy_sems(2)],
        (*terms_row, *terms_col, back),
    )
    pieces = swap(terms.reshape(16, 2, 24, HALF_WIDTH), ("dp", "ctx"), plane_groups())
    own = call(
        group_sum_kernel,
        shape(8, 2, 24, HALF_WIDTH),
        10 ** 9,
        [buffer(16, 2, 24, HALF_WIDTH), buffer(2, 24, HALF_WIDTH), copy_sems(9)],
        (pieces,),
    )
    whole = swap(own, "ctx")
    factor = (lax.axis_size("dp") * lax.axis_size("ctx") * POSITIONS) ** (-0.5)
    qkv_grad, out_grad = call(
        functools.partial(assemble_kernel, factor),
        (shape(48, 3 * WIDTH, dtype=F32), shape(48, WIDTH, dtype=F32)),
        10 ** 6,
        [
            buffer(8, 2, 24, HALF_WIDTH),
            buffer(48, 3 * WIDTH, dtype=F32),
            buffer(48, WIDTH, dtype=F32),
            copy_sems(3),
        ],
        (whole,),
    )
    return (attention_out[None], normed_grad[None], qkv_grad, out_grad)


def solution(mesh):
    placed = (P("dp", "ctx", None), P("dp", "ctx", None), P(), P())
    return jax.shard_map(
        body,
        mesh=mesh,
        in_specs=placed,
        out_specs=(P("dp", "ctx", None), P("dp", "ctx", None), P("dp", None), P("dp", None)),
        check_vma=False,
    )
```

```python
import functools

import jax
import jax.numpy as jnp
from jax import lax
from jax.experimental import pallas as pl
from jax.experimental.pallas import tpu as pltpu
from jax.sharding import PartitionSpec as P

WIDTH = 768
HALF_WIDTH = 384
HEAD_DIM = 64
POSITIONS = 512
ROWS = 8
COLUMNS = 64
PAIR = 128
PAIRS = HALF_WIDTH // PAIR
BLOCK = 256
CHUNK = 16
BF = jnp.bfloat16
F32 = jnp.float32
MIB = 1024 * 1024


def dot(a, b):
    return lax.dot_general(a, b, (((1,), (0,)), ((), ())), preferred_element_type=F32)


def dot_nt(a, b):
    return lax.dot_general(a, b, (((1,), (1,)), ((), ())), preferred_element_type=F32)


def dot_tn(a, b):
    return lax.dot_general(a, b, (((0,), (0,)), ((), ())), preferred_element_type=F32)


def half_lanes(array, half):
    lane = lax.broadcasted_iota(jnp.int32, array.shape, array.ndim - 1)
    inside = (lane >= HEAD_DIM) if half else (lane < HEAD_DIM)
    return jnp.where(inside, array, jnp.zeros_like(array))


def probabilities(scores, start):
    square = scores[:, start:]
    row = lax.broadcasted_iota(jnp.int32, square.shape, 0)
    square = jnp.where(lax.broadcasted_iota(jnp.int32, square.shape, 1) <= row, square, -1e30)
    scores = jnp.concatenate([scores[:, :start], square], axis=1) if start else square
    top = jnp.max(scores, axis=-1, keepdims=True)
    weights = jnp.exp(scores - top)
    return weights * (1.0 / jnp.sum(weights, axis=-1, keepdims=True))


def chunk_probabilities(scores, allowed):
    scores = jnp.where(allowed, scores, -1e30)
    top = jnp.max(scores, axis=-1, keepdims=True)
    weights = jnp.exp(scores - top)
    return weights * (1.0 / jnp.sum(weights, axis=-1, keepdims=True))


def load(x_hbm, c_hbm, qkv_hbm, out_hbm, x, c, w_qkv, w_out, sems, first):
    copies = [pltpu.make_async_copy(x_hbm, x, sems.at[0])]
    for part in range(3):
        columns = pl.ds(part * WIDTH + first, HALF_WIDTH)
        place = pl.ds(part * HALF_WIDTH, HALF_WIDTH)
        copies.append(pltpu.make_async_copy(qkv_hbm.at[:, columns], w_qkv.at[:, place], sems.at[1 + part]))
    copies.append(pltpu.make_async_copy(c_hbm, c, sems.at[4]))
    copies.append(pltpu.make_async_copy(out_hbm.at[:, pl.ds(first, HALF_WIDTH)], w_out, sems.at[5]))
    for copy in copies:
        copy.start()
    return copies


def project(copies, x, c, w_qkv, w_out, proj, gctx):
    copies[0].wait()
    for part in range(3):
        copies[1 + part].wait()
        columns = slice(part * HALF_WIDTH, (part + 1) * HALF_WIDTH)
        piece = dot(x[...].reshape(POSITIONS, WIDTH), w_qkv[:, columns]).astype(BF)
        if part == 0:
            piece = piece * BF(HEAD_DIM ** -0.5)
        proj[:, columns] = piece
    copies[4].wait()
    copies[5].wait()
    gctx[...] = dot(c[...].reshape(POSITIONS, WIDTH), w_out[...]).astype(BF)


def weight_terms(x, c, grads, ctx, terms, targets, sems, extra):
    copies = []
    for part in range(4):
        for index, (place, target) in enumerate(targets):
            copies.append(
                pltpu.make_async_copy(terms.at[:, place, part], target.at[:, part], sems.at[2 + 4 * index + part])
            )
    extra = start_all(
        [pltpu.make_async_copy(source, target, sems.at[index]) for index, (source, target) in enumerate(extra)]
    )
    x_t = jnp.transpose(x[...].reshape(POSITIONS, WIDTH))
    for part in range(3):
        res = dot(x_t, grads[:, part * HALF_WIDTH : (part + 1) * HALF_WIDTH]).astype(BF)
        terms[:, :, part] = res.reshape(ROWS, 2, 48, HALF_WIDTH)
        copies[2 * part].start()
        copies[2 * part + 1].start()
    c_t = jnp.transpose(c[...].reshape(POSITIONS, WIDTH))
    terms[:, :, 3] = dot(c_t, ctx[...]).astype(BF).reshape(ROWS, 2, 48, HALF_WIDTH)
    copies[6].start()
    copies[7].start()
    wait_all(extra + copies)


def row_kernel(
    core_ref, x_hbm, c_hbm, qkv_hbm, out_hbm, grads_hbm, ctx_hbm, keep_hbm, send_hbm,
    x, c, w_qkv, w_out, proj, gctx, grads, ctx, terms, sems, probs, dscores,
):
    copies = load(x_hbm, c_hbm, qkv_hbm, out_hbm, x, c, w_qkv, w_out, sems, 0)
    project(copies, x, c, w_qkv, w_out, proj, gctx)
    def products(pair, start):
        lanes = slice(pair * PAIR, (pair + 1) * PAIR)
        stop = start + BLOCK
        query, grad = proj[start:stop, lanes], gctx[start:stop, lanes]
        keys = [half_lanes(proj[:stop, HALF_WIDTH + pair * PAIR : HALF_WIDTH + (pair + 1) * PAIR], h) for h in range(2)]
        values = [
            half_lanes(proj[:stop, 2 * HALF_WIDTH + pair * PAIR : 2 * HALF_WIDTH + (pair + 1) * PAIR], h)
            for h in range(2)
        ]
        scores = [dot_nt(query, key) for key in keys]
        return pair, start, keys, values, scores, [dot_nt(grad, value) for value in values]

    def softmax(pair, start, keys, values, scores, grad_weights):
        lanes = slice(pair * PAIR, (pair + 1) * PAIR)
        stop = start + BLOCK
        outs, dqs = [], []
        weights = [probabilities(scores[half], start) for half in range(2)]
        for half in range(2):
            rounded = weights[half].astype(BF)
            probs[pair, half, start:stop, :stop] = rounded
            outs.append(dot(rounded, values[half]))
            delta = jnp.sum(weights[half] * grad_weights[half], axis=-1, keepdims=True)
            ds = (weights[half] * (grad_weights[half] - delta)).astype(BF)
            dscores[pair, half, start:stop, :stop] = ds
            dqs.append(dot(ds, keys[half]))
        ctx[start:stop, lanes] = (outs[0] + outs[1]).astype(BF)
        grads[start:stop, lanes] = ((dqs[0] + dqs[1]) * (HEAD_DIM ** -0.5)).astype(BF)

    def key_sums(pair):
        lanes = slice(pair * PAIR, (pair + 1) * PAIR)
        k_lanes = slice(HALF_WIDTH + pair * PAIR, HALF_WIDTH + (pair + 1) * PAIR)
        v_lanes = slice(2 * HALF_WIDTH + pair * PAIR, 2 * HALF_WIDTH + (pair + 1) * PAIR)
        query_t = jnp.transpose(proj[:, lanes])
        grad_t = jnp.transpose(gctx[:, lanes])
        for start in range(0, POSITIONS, BLOCK):
            stop = start + BLOCK
            for place, left, right in ((k_lanes, query_t, dscores), (v_lanes, grad_t, probs)):
                both = jnp.concatenate(
                    [
                        dot(left[half * HEAD_DIM : (half + 1) * HEAD_DIM, start:], right[pair, half, start:, start:stop])
                        for half in range(2)
                    ],
                    axis=0,
                )
                grads[start:stop, place] = jnp.transpose(both.astype(BF))

    order = [(pair, start) for pair in range(PAIRS) for start in range(0, POSITIONS, BLOCK)]
    held = products(*order[0])
    for index, (pair, start) in enumerate(order):
        following = products(*order[index + 1]) if index + 1 < len(order) else None
        softmax(*held)
        held = following
        if start and pair:
            key_sums(pair - 1)
    key_sums(PAIRS - 1)
    core = core_ref[0]
    targets = [(1 - core, send_hbm), (core, keep_hbm)]
    weight_terms(x, c, grads, ctx, terms, targets, sems, [(grads, grads_hbm), (ctx, ctx_hbm)])


def column_kernel(
    core_ref, both_hbm, qkv_hbm, out_hbm, after, back_hbm, keep_hbm, send_hbm,
    x, c, w_qkv, w_out, proj, gctx, grads, ctx, terms, sems, back,
):
    x_hbm, c_hbm = both_hbm.at[:, 0], both_hbm.at[:, 1]
    copies = load(x_hbm, c_hbm, qkv_hbm, out_hbm, x, c, w_qkv, w_out, sems, HALF_WIDTH)
    project(copies, x, c, w_qkv, w_out, proj, gctx)
    size = ROWS * CHUNK
    chunks = COLUMNS // CHUNK
    line = lax.broadcasted_iota(jnp.int32, (size, size), 0)
    across = lax.broadcasted_iota(jnp.int32, (size, size), 1)
    allowed = ((line % CHUNK) == (across % CHUNK)) & (across <= line)
    allowed = jnp.concatenate([allowed.astype(F32)] * chunks, axis=0) > 0

    def twice(array):
        return jnp.concatenate([half_lanes(array, 0), half_lanes(array, 1)], axis=0)

    def gather(ref, base):
        whole = ref[:, base : base + PAIR].reshape(ROWS, COLUMNS, PAIR)
        return [
            whole[:, t * CHUNK : (t + 1) * CHUNK].reshape(size, PAIR) for t in range(chunks)
        ]

    def scatter(ref, base, pieces):
        whole = jnp.concatenate([p.reshape(ROWS, CHUNK, PAIR) for p in pieces], axis=1)
        ref[:, base : base + PAIR] = whole.reshape(POSITIONS, PAIR)

    def products(pair):
        base = pair * PAIR
        query, key, value = [gather(proj, part * HALF_WIDTH + base) for part in range(3)]
        grad = gather(gctx, base)
        keys, values, queries, grad_parts = [[twice(t) for t in part] for part in (key, value, query, grad)]
        scores = jnp.concatenate([dot_nt(a, b) for a, b in zip(query, keys)], axis=0)
        grad_weights = jnp.concatenate([dot_nt(a, b) for a, b in zip(grad, values)], axis=0)
        return base, keys, values, queries, grad_parts, scores, grad_weights

    def finish(base, keys, values, queries, grad_parts, scores, grad_weights):
        rounded, dscores = [], []
        for half in range(2):
            lanes = slice(half * size, (half + 1) * size)
            weights = chunk_probabilities(scores[:, lanes], allowed)
            rounded.append(weights.astype(BF))
            part = grad_weights[:, lanes]
            delta = jnp.sum(weights * part, axis=-1, keepdims=True)
            dscores.append((weights * (part - delta)).astype(BF))
        outs, dqs, dks, dvs = [], [], [], []
        for t in range(chunks):
            rows = slice(t * size, (t + 1) * size)
            wide = [jnp.concatenate([pieces[0][rows], pieces[1][rows]], axis=1) for pieces in (rounded, dscores)]
            tall = [jnp.concatenate([pieces[0][rows], pieces[1][rows]], axis=0) for pieces in (rounded, dscores)]
            outs.append(dot(wide[0], values[t]).astype(BF))
            dqs.append((dot(wide[1], keys[t]) * (HEAD_DIM ** -0.5)).astype(BF))
            dks.append(dot_tn(tall[1], queries[t]).astype(BF))
            dvs.append(dot_tn(tall[0], grad_parts[t]).astype(BF))
        scatter(ctx, base, outs)
        scatter(grads, base, dqs)
        scatter(grads, HALF_WIDTH + base, dks)
        scatter(grads, 2 * HALF_WIDTH + base, dvs)

    for item in [products(pair) for pair in range(PAIRS)]:
        finish(*item)
    core = core_ref[0]
    targets = [(1 - core, send_hbm), (core, keep_hbm)]
    back[:, WIDTH:] = ctx[...]
    for start in range(0, WIDTH, BLOCK):
        columns = slice(start, start + BLOCK)
        back[:, columns] = dot_nt(grads[...], w_qkv[columns]).astype(BF)
    weight_terms(x, c, grads, ctx, terms, targets, sems, [(back, back_hbm)])


def wait_all(copies):
    for copy in copies:
        copy.wait()


def start_all(copies):
    for copy in copies:
        copy.start()
    return copies


def weight_copies(qkv_hbm, w_qkv, sems, first):
    return [
        pltpu.make_async_copy(
            qkv_hbm.at[:, pl.ds(part * WIDTH + first, HALF_WIDTH)], w_qkv.at[part], sems.at[part]
        )
        for part in range(3)
    ]


def grads_times_weights(grads, w_qkv, columns):
    return sum(
        dot_nt(grads[:, part * HALF_WIDTH : (part + 1) * HALF_WIDTH], w_qkv[part, columns]) for part in range(3)
    )


def final_kernel(
    grads_hbm, ctx_hbm, back_hbm, qkv_hbm, out_hbm, attention_hbm, normed_hbm,
    grads, ctx, back, w_qkv, w_out, attention, normed, sems, out_sems,
):
    ins = start_all(
        [
            pltpu.make_async_copy(source, target, sems.at[3 + index])
            for index, (source, target) in enumerate(
                ((ctx_hbm, ctx), (back_hbm, back), (out_hbm, w_out), (grads_hbm, grads))
            )
        ]
        + weight_copies(qkv_hbm, w_qkv, sems, 0)
    )
    outs = []
    wait_all(ins[:3])
    for index in range(3):
        columns = slice(index * BLOCK, (index + 1) * BLOCK)
        span = pl.ds(index * BLOCK, BLOCK)
        attention[:, columns] = (
            dot_nt(ctx[...], w_out[columns, :HALF_WIDTH]) + dot_nt(back[:, WIDTH:], w_out[columns, HALF_WIDTH:])
        ).astype(BF)
        outs += start_all(
            [pltpu.make_async_copy(attention.at[:, span], attention_hbm.at[:, span], out_sems.at[0, index])]
        )
    wait_all(ins[3:])
    for index in range(3):
        columns = slice(index * BLOCK, (index + 1) * BLOCK)
        span = pl.ds(index * BLOCK, BLOCK)
        normed[:, columns] = (
            back[:, columns].astype(F32) + grads_times_weights(grads, w_qkv, columns)
        ).astype(BF)
        outs += start_all([pltpu.make_async_copy(normed.at[:, span], normed_hbm.at[:, span], out_sems.at[1, index])])
    wait_all(outs)


def order_kernel(back_hbm, first, second, third, out_hbm, zeros, sems):
    zeros[...] = jnp.zeros_like(zeros)
    wait_all(start_all([pltpu.make_async_copy(zeros, out_hbm, sems.at[0])]))


def pack_kernel(x_hbm, c_hbm, both_hbm, both, sems, out_sems):
    spans = [pl.ds(2 * index, 2) for index in range(4)]
    ins = start_all(
        [
            pltpu.make_async_copy(source.at[span], both.at[span, place], sems.at[place, index])
            for index, span in enumerate(spans)
            for place, source in enumerate((x_hbm, c_hbm))
        ]
    )
    outs = []
    for index, span in enumerate(spans):
        wait_all(ins[2 * index : 2 * index + 2])
        outs += start_all([pltpu.make_async_copy(both.at[span], both_hbm.at[span], out_sems.at[index])])
    wait_all(outs)


def pair_sum_kernel(x_ref, keep_hbm, received_hbm, *refs):
    out_hbms = refs[-8:-4]
    terms, totals, sems, out_sems = refs[-4:]
    ins, outs = [], []
    order = (1, 3, 2, 0)
    for step in order:
        place = pl.ds(2 * lax.rem(x_ref[0] + step, 4), 2)
        for index, source in enumerate((keep_hbm, received_hbm)):
            ins += start_all(
                [pltpu.make_async_copy(source.at[place], terms.at[step, index], sems.at[index, step])]
            )
    for index, step in enumerate(order):
        wait_all(ins[2 * index : 2 * index + 2])
        totals[step] = (terms[step, 0].astype(F32) + terms[step, 1].astype(F32)).astype(BF)
        outs += start_all([pltpu.make_async_copy(totals.at[step], out_hbms[step], out_sems.at[step])])
    wait_all(outs)


def ring_sum_kernel(*refs):
    in_hbms, (out_hbm, terms, totals, sems, out_sems) = refs[:8], refs[9:]
    ins = [
        start_all(
            [
                pltpu.make_async_copy(source.at[z_hi], terms.at[index, z_hi], sems.at[index, z_hi])
                for index, source in enumerate(in_hbms)
            ]
        )
        for z_hi in range(2)
    ]
    outs = []
    for z_hi in range(2):
        wait_all(ins[z_hi])
        for half in range(2):
            total = sum(terms[4 * half + step, z_hi].astype(F32) for step in range(4))
            for z_lo in range(2):
                totals[z_hi, :, z_lo, half] = total[:, 24 * z_lo : 24 * z_lo + 24].astype(BF)
        outs += start_all([pltpu.make_async_copy(totals.at[z_hi], out_hbm.at[z_hi], out_sems.at[z_hi])])
    wait_all(outs)


def group_sum_kernel(pieces_hbm, after, out_hbm, pieces, total, sems, in_sems):
    ins = start_all(
        [
            pltpu.make_async_copy(pieces_hbm.at[pl.ds(4 * index, 4)], pieces.at[pl.ds(4 * index, 4)], in_sems.at[index])
            for index in range(4)
        ]
    )
    parts = []
    for index in range(4):
        ins[index].wait()
        parts.append(jnp.sum(pieces[4 * index : 4 * index + 4].astype(F32), axis=0))
    total[...] = sum(parts).astype(BF)
    wait_all(
        start_all([pltpu.make_async_copy(total, out_hbm.at[place], sems.at[place]) for place in range(8)])
    )


def assemble_kernel(factor, whole_hbm, qkv_hbm, out_hbm, whole, qkv_grad, out_grad, sems):
    ins = start_all(
        [
            pltpu.make_async_copy(whole_hbm.at[pl.ds(4 * z_lo, 4)], whole.at[pl.ds(4 * z_lo, 4)], sems.at[0, z_lo])
            for z_lo in range(2)
        ]
    )
    outs = []
    for z_lo in range(2):
        ins[z_lo].wait()
        rows, span = slice(24 * z_lo, 24 * z_lo + 24), pl.ds(24 * z_lo, 24)
        for part in range(4):
            for half in range(2):
                value = whole[4 * z_lo + part, half].astype(F32) * factor
                start = half * HALF_WIDTH
                if part < 3:
                    start += part * WIDTH
                    qkv_grad[rows, start : start + HALF_WIDTH] = value
                else:
                    out_grad[rows, start : start + HALF_WIDTH] = value
        outs += start_all(
            [
                pltpu.make_async_copy(qkv_grad.at[span], qkv_hbm.at[span], sems.at[1, z_lo]),
                pltpu.make_async_copy(out_grad.at[span], out_hbm.at[span], sems.at[2, z_lo]),
            ]
        )
    wait_all(outs)


SMEM = pl.BlockSpec(memory_space=pltpu.SMEM)
HBM = pl.BlockSpec(memory_space=pltpu.HBM)


def buffer(*dims, dtype=BF):
    return pltpu.VMEM(dims, dtype)


def copy_sems(*dims):
    return pltpu.SemaphoreType.DMA(dims)


def shape(*dims, dtype=BF):
    return jax.ShapeDtypeStruct(dims, dtype)


def call(kernel, out_shape, flops, scratch, arrays, mib=64):
    scalars = sum(1 for array in arrays if array.ndim == 1)
    return pl.pallas_call(
        kernel,
        out_shape=out_shape,
        in_specs=[SMEM] * scalars + [HBM] * (len(arrays) - scalars),
        out_specs=jax.tree.map(lambda _: HBM, out_shape),
        scratch_shapes=scratch,
        compiler_params=pltpu.CompilerParams(vmem_limit_bytes=mib * MIB),
        cost_estimate=pl.CostEstimate(flops=flops, bytes_accessed=2 ** 16, transcendentals=0),
    )(*arrays)


def sublayer(kernel, dims, out_shapes, scratch, *arrays):
    return call(
        kernel,
        (*out_shapes, shape(ROWS, 4, 48, HALF_WIDTH), shape(ROWS, 4, 48, HALF_WIDTH)),
        2 * 10 ** 10,
        [
            buffer(*dims),
            buffer(*dims),
            buffer(WIDTH, 3 * HALF_WIDTH),
            buffer(WIDTH, HALF_WIDTH),
            buffer(POSITIONS, 3 * HALF_WIDTH),
            buffer(POSITIONS, HALF_WIDTH),
            buffer(POSITIONS, 3 * HALF_WIDTH),
            buffer(POSITIONS, HALF_WIDTH),
            buffer(ROWS, 2, 4, 48, HALF_WIDTH),
            copy_sems(10),
            *scratch,
        ],
        arrays,
        mib=64,
    )


def swap(part, axis, groups=None):
    return lax.all_to_all(part, axis, split_axis=0, concat_axis=0, tiled=True, axis_index_groups=groups)


def plane_groups():
    def flat(x, z_hi, core, z_lo, y):
        return ((x * 2 + z_hi) * 2 + core) * 8 + z_lo * 4 + y

    return [
        [flat(x, z_hi, core, z_lo, y) for z_hi in range(2) for y in range(4) for z_lo in range(2)]
        for x in range(4)
        for core in range(2)
    ]


def exchange(send):
    return lax.ppermute(send, "dp", [(i, i ^ 1) for i in range(16)])


def pair_sum(x_index, keep, send, *after):
    return call(
        pair_sum_kernel,
        (shape(2, 4, 48, HALF_WIDTH),) * 4,
        2 * 10 ** 9,
        [buffer(4, 2, 2, 4, 48, HALF_WIDTH), buffer(4, 2, 4, 48, HALF_WIDTH), copy_sems(2, 4), copy_sems(4)],
        (x_index, keep, exchange(send), *after),
    )


def ring(parts):
    return [parts[0]] + [
        lax.ppermute(parts[step], "dp", [(i, (i + 4 * step) % 16) for i in range(16)]) for step in range(1, 4)
    ]


def body(normed, cotangent, qkv_weight, out_weight):
    x, c = normed[0], cotangent[0]
    dp = lax.axis_index("dp")
    core = (dp % 2).reshape(1)
    x_index = (dp // 4).reshape(1)
    grid_dims = (ROWS, COLUMNS, WIDTH)
    both = call(
        pack_kernel,
        shape(ROWS, 2, COLUMNS, WIDTH),
        10 ** 6,
        [buffer(ROWS, 2, COLUMNS, WIDTH), copy_sems(2, 4), copy_sems(4)],
        (x.reshape(grid_dims), c.reshape(grid_dims)),
    )
    both = swap(both, "ctx")
    grads_row, ctx_row, keep_row, send_row = sublayer(
        row_kernel,
        (POSITIONS, WIDTH),
        [shape(POSITIONS, 3 * HALF_WIDTH), shape(POSITIONS, HALF_WIDTH)],
        [buffer(PAIRS, 2, POSITIONS, POSITIONS)] * 2,
        core, x, c, qkv_weight, out_weight,
    )
    terms_row = ring(pair_sum(x_index, keep_row, send_row))
    back_width = WIDTH + HALF_WIDTH
    back, keep_col, send_col = sublayer(
        column_kernel,
        grid_dims,
        [shape(POSITIONS, back_width)],
        [buffer(POSITIONS, back_width)],
        core, both, qkv_weight, out_weight, terms_row[0],
    )
    order = call(order_kernel, shape(8, PAIR, dtype=F32), 4 * 10 ** 10, [buffer(8, PAIR, dtype=F32), copy_sems(1)], (back, *terms_row[1:]))
    parts = pair_sum(x_index, keep_col, send_col, order)
    terms_col = ring(parts)
    back = swap(back.reshape(ROWS, COLUMNS, back_width), "ctx").reshape(POSITIONS, back_width)
    attention_out, normed_grad = call(
        final_kernel,
        (shape(POSITIONS, WIDTH),) * 2,
        4 * 10 ** 9,
        [
            buffer(POSITIONS, 3 * HALF_WIDTH),
            buffer(POSITIONS, HALF_WIDTH),
            buffer(POSITIONS, back_width),
            buffer(3, WIDTH, HALF_WIDTH),
            buffer(WIDTH, WIDTH),
            buffer(POSITIONS, WIDTH),
            buffer(POSITIONS, WIDTH),
            copy_sems(7),
            copy_sems(2, 4),
        ],
        (grads_row, ctx_row, back, qkv_weight, out_weight),
        mib=64,
    )
    terms = call(
        ring_sum_kernel,
        shape(2, 4, 2, 2, 24, HALF_WIDTH),
        2 * 10 ** 9,
        [buffer(8, 2, 4, 48, HALF_WIDTH), buffer(2, 4, 2, 2, 24, HALF_WIDTH), copy_sems(8, 2), copy_sems(2)],
        (*terms_row, *terms_col, back),
    )
    pieces = swap(terms.reshape(16, 2, 24, HALF_WIDTH), ("dp", "ctx"), plane_groups())
    own = call(
        group_sum_kernel,
        shape(8, 2, 24, HALF_WIDTH),
        10 ** 9,
        [buffer(16, 2, 24, HALF_WIDTH), buffer(2, 24, HALF_WIDTH), copy_sems(8), copy_sems(4)],
        (pieces, attention_out),
    )
    whole = swap(own, "ctx")
    factor = (lax.axis_size("dp") * lax.axis_size("ctx") * POSITIONS) ** (-0.5)
    qkv_grad, out_grad = call(
        functools.partial(assemble_kernel, factor),
        (shape(48, 3 * WIDTH, dtype=F32), shape(48, WIDTH, dtype=F32)),
        10 ** 6,
        [
            buffer(8, 2, 24, HALF_WIDTH),
            buffer(48, 3 * WIDTH, dtype=F32),
            buffer(48, WIDTH, dtype=F32),
            copy_sems(3, 2),
        ],
        (whole,),
    )
    return (attention_out[None], normed_grad[None], qkv_grad, out_grad)


def solution(mesh):
    placed = (P("dp", "ctx", None), P("dp", "ctx", None), P(), P())
    return jax.shard_map(
        body,
        mesh=mesh,
        in_specs=placed,
        out_specs=(P("dp", "ctx", None), P("dp", "ctx", None), P("dp", None), P("dp", None)),
        check_vma=False,
    )
```

```python
import functools

import jax
import jax.numpy as jnp
from jax import lax
from jax.experimental import pallas as pl
from jax.experimental.pallas import tpu as pltpu
from jax.sharding import PartitionSpec as P

WIDTH = 768
HALF_WIDTH = 384
HEAD_DIM = 64
POSITIONS = 512
ROWS = 8
COLUMNS = 64
PAIR = 128
PAIRS = HALF_WIDTH // PAIR
BLOCK = 256
CHUNK = 16
BF = jnp.bfloat16
F32 = jnp.float32
MIB = 1024 * 1024


def dot(a, b):
    return lax.dot_general(a, b, (((1,), (0,)), ((), ())), preferred_element_type=F32)


def dot_nt(a, b):
    return lax.dot_general(a, b, (((1,), (1,)), ((), ())), preferred_element_type=F32)


def dot_tn(a, b):
    return lax.dot_general(a, b, (((0,), (0,)), ((), ())), preferred_element_type=F32)


def half_lanes(array, half):
    lane = lax.broadcasted_iota(jnp.int32, array.shape, array.ndim - 1)
    inside = (lane >= HEAD_DIM) if half else (lane < HEAD_DIM)
    return jnp.where(inside, array, jnp.zeros_like(array))


def probabilities(scores, start):
    square = scores[:, start:]
    row = lax.broadcasted_iota(jnp.int32, square.shape, 0)
    square = jnp.where(lax.broadcasted_iota(jnp.int32, square.shape, 1) <= row, square, -1e30)
    scores = jnp.concatenate([scores[:, :start], square], axis=1) if start else square
    top = jnp.max(scores, axis=-1, keepdims=True)
    weights = jnp.exp(scores - top)
    return weights * (1.0 / jnp.sum(weights, axis=-1, keepdims=True))


def chunk_probabilities(scores, allowed):
    scores = jnp.where(allowed, scores, -1e30)
    top = jnp.max(scores, axis=-1, keepdims=True)
    weights = jnp.exp(scores - top)
    return weights * (1.0 / jnp.sum(weights, axis=-1, keepdims=True))


def load(x_hbm, c_hbm, qkv_hbm, out_hbm, x, c, w_qkv, w_out, sems, first):
    copies = [pltpu.make_async_copy(x_hbm, x, sems.at[0])]
    for part in range(3):
        columns = pl.ds(part * WIDTH + first, HALF_WIDTH)
        place = pl.ds(part * HALF_WIDTH, HALF_WIDTH)
        copies.append(pltpu.make_async_copy(qkv_hbm.at[:, columns], w_qkv.at[:, place], sems.at[1 + part]))
    copies.append(pltpu.make_async_copy(c_hbm, c, sems.at[4]))
    copies.append(pltpu.make_async_copy(out_hbm.at[:, pl.ds(first, HALF_WIDTH)], w_out, sems.at[5]))
    for copy in copies:
        copy.start()
    return copies


def project(copies, x, c, w_qkv, w_out, proj, gctx):
    copies[0].wait()
    for part in range(3):
        copies[1 + part].wait()
        columns = slice(part * HALF_WIDTH, (part + 1) * HALF_WIDTH)
        piece = dot(x[...].reshape(POSITIONS, WIDTH), w_qkv[:, columns]).astype(BF)
        if part == 0:
            piece = piece * BF(HEAD_DIM ** -0.5)
        proj[:, columns] = piece
    copies[4].wait()
    copies[5].wait()
    gctx[...] = dot(c[...].reshape(POSITIONS, WIDTH), w_out[...]).astype(BF)


def weight_terms(x, c, grads, ctx, terms, targets, sems, extra):
    copies = []
    for part in range(4):
        for index, (place, target) in enumerate(targets):
            copies.append(
                pltpu.make_async_copy(terms.at[:, place, part], target.at[:, part], sems.at[2 + 4 * index + part])
            )
    extra = start_all(
        [pltpu.make_async_copy(source, target, sems.at[index]) for index, (source, target) in enumerate(extra)]
    )
    x_t = jnp.transpose(x[...].reshape(POSITIONS, WIDTH))
    for part in range(3):
        res = dot(x_t, grads[:, part * HALF_WIDTH : (part + 1) * HALF_WIDTH]).astype(BF)
        terms[:, :, part] = res.reshape(ROWS, 2, 48, HALF_WIDTH)
        copies[2 * part].start()
        copies[2 * part + 1].start()
    c_t = jnp.transpose(c[...].reshape(POSITIONS, WIDTH))
    terms[:, :, 3] = dot(c_t, ctx[...]).astype(BF).reshape(ROWS, 2, 48, HALF_WIDTH)
    copies[6].start()
    copies[7].start()
    wait_all(extra + copies)


def row_kernel(
    core_ref, x_hbm, c_hbm, qkv_hbm, out_hbm, grads_hbm, ctx_hbm, keep_hbm, send_hbm,
    x, c, w_qkv, w_out, proj, gctx, grads, ctx, terms, sems, probs, dscores,
):
    copies = load(x_hbm, c_hbm, qkv_hbm, out_hbm, x, c, w_qkv, w_out, sems, 0)
    project(copies, x, c, w_qkv, w_out, proj, gctx)
    def products(pair, start):
        lanes = slice(pair * PAIR, (pair + 1) * PAIR)
        stop = start + BLOCK
        query, grad = proj[start:stop, lanes], gctx[start:stop, lanes]
        keys = [half_lanes(proj[:stop, HALF_WIDTH + pair * PAIR : HALF_WIDTH + (pair + 1) * PAIR], h) for h in range(2)]
        values = [
            half_lanes(proj[:stop, 2 * HALF_WIDTH + pair * PAIR : 2 * HALF_WIDTH + (pair + 1) * PAIR], h)
            for h in range(2)
        ]
        scores = [dot_nt(query, key) for key in keys]
        return pair, start, keys, values, scores, [dot_nt(grad, value) for value in values]

    def softmax(pair, start, keys, values, scores, grad_weights):
        lanes = slice(pair * PAIR, (pair + 1) * PAIR)
        stop = start + BLOCK
        outs, dqs = [], []
        weights = [probabilities(scores[half], start) for half in range(2)]
        for half in range(2):
            rounded = weights[half].astype(BF)
            probs[pair, half, start:stop, :stop] = rounded
            outs.append(dot(rounded, values[half]))
            delta = jnp.sum(weights[half] * grad_weights[half], axis=-1, keepdims=True)
            ds = (weights[half] * (grad_weights[half] - delta)).astype(BF)
            dscores[pair, half, start:stop, :stop] = ds
            dqs.append(dot(ds, keys[half]))
        ctx[start:stop, lanes] = (outs[0] + outs[1]).astype(BF)
        grads[start:stop, lanes] = ((dqs[0] + dqs[1]) * (HEAD_DIM ** -0.5)).astype(BF)

    def key_sums(pair):
        lanes = slice(pair * PAIR, (pair + 1) * PAIR)
        k_lanes = slice(HALF_WIDTH + pair * PAIR, HALF_WIDTH + (pair + 1) * PAIR)
        v_lanes = slice(2 * HALF_WIDTH + pair * PAIR, 2 * HALF_WIDTH + (pair + 1) * PAIR)
        query_t = jnp.transpose(proj[:, lanes])
        grad_t = jnp.transpose(gctx[:, lanes])
        for start in range(0, POSITIONS, BLOCK):
            stop = start + BLOCK
            for place, left, right in ((k_lanes, query_t, dscores), (v_lanes, grad_t, probs)):
                both = jnp.concatenate(
                    [
                        dot(left[half * HEAD_DIM : (half + 1) * HEAD_DIM, start:], right[pair, half, start:, start:stop])
                        for half in range(2)
                    ],
                    axis=0,
                )
                grads[start:stop, place] = jnp.transpose(both.astype(BF))

    order = [(pair, start) for pair in range(PAIRS) for start in range(0, POSITIONS, BLOCK)]
    held = products(*order[0])
    for index, (pair, start) in enumerate(order):
        following = products(*order[index + 1]) if index + 1 < len(order) else None
        softmax(*held)
        held = following
        if start and pair:
            key_sums(pair - 1)
    key_sums(PAIRS - 1)
    core = core_ref[0]
    targets = [(1 - core, send_hbm), (core, keep_hbm)]
    weight_terms(x, c, grads, ctx, terms, targets, sems, [(grads, grads_hbm), (ctx, ctx_hbm)])


def column_kernel(
    core_ref, both_hbm, qkv_hbm, out_hbm, after, back_hbm, keep_hbm, send_hbm,
    x, c, w_qkv, w_out, proj, gctx, grads, ctx, terms, sems, back,
):
    x_hbm, c_hbm = both_hbm.at[:, 0], both_hbm.at[:, 1]
    copies = load(x_hbm, c_hbm, qkv_hbm, out_hbm, x, c, w_qkv, w_out, sems, HALF_WIDTH)
    project(copies, x, c, w_qkv, w_out, proj, gctx)
    size = ROWS * CHUNK
    chunks = COLUMNS // CHUNK
    line = lax.broadcasted_iota(jnp.int32, (size, size), 0)
    across = lax.broadcasted_iota(jnp.int32, (size, size), 1)
    allowed = ((line % CHUNK) == (across % CHUNK)) & (across <= line)
    allowed = jnp.concatenate([allowed.astype(F32)] * chunks, axis=0) > 0

    def twice(array):
        return jnp.concatenate([half_lanes(array, 0), half_lanes(array, 1)], axis=0)

    def gather(ref, base):
        whole = ref[:, base : base + PAIR].reshape(ROWS, COLUMNS, PAIR)
        return [
            whole[:, t * CHUNK : (t + 1) * CHUNK].reshape(size, PAIR) for t in range(chunks)
        ]

    def scatter(ref, base, pieces):
        whole = jnp.concatenate([p.reshape(ROWS, CHUNK, PAIR) for p in pieces], axis=1)
        ref[:, base : base + PAIR] = whole.reshape(POSITIONS, PAIR)

    def products(pair):
        base = pair * PAIR
        query, key, value = [gather(proj, part * HALF_WIDTH + base) for part in range(3)]
        grad = gather(gctx, base)
        keys, values, queries, grad_parts = [[twice(t) for t in part] for part in (key, value, query, grad)]
        scores = jnp.concatenate([dot_nt(a, b) for a, b in zip(query, keys)], axis=0)
        grad_weights = jnp.concatenate([dot_nt(a, b) for a, b in zip(grad, values)], axis=0)
        return base, keys, values, queries, grad_parts, scores, grad_weights

    def finish(base, keys, values, queries, grad_parts, scores, grad_weights):
        rounded, dscores = [], []
        for half in range(2):
            lanes = slice(half * size, (half + 1) * size)
            weights = chunk_probabilities(scores[:, lanes], allowed)
            rounded.append(weights.astype(BF))
            part = grad_weights[:, lanes]
            delta = jnp.sum(weights * part, axis=-1, keepdims=True)
            dscores.append((weights * (part - delta)).astype(BF))
        outs, dqs, dks, dvs = [], [], [], []
        for t in range(chunks):
            rows = slice(t * size, (t + 1) * size)
            wide = [jnp.concatenate([pieces[0][rows], pieces[1][rows]], axis=1) for pieces in (rounded, dscores)]
            tall = [jnp.concatenate([pieces[0][rows], pieces[1][rows]], axis=0) for pieces in (rounded, dscores)]
            outs.append(dot(wide[0], values[t]).astype(BF))
            dqs.append((dot(wide[1], keys[t]) * (HEAD_DIM ** -0.5)).astype(BF))
            dks.append(dot_tn(tall[1], queries[t]).astype(BF))
            dvs.append(dot_tn(tall[0], grad_parts[t]).astype(BF))
        scatter(ctx, base, outs)
        scatter(grads, base, dqs)
        scatter(grads, HALF_WIDTH + base, dks)
        scatter(grads, 2 * HALF_WIDTH + base, dvs)

    for item in [products(pair) for pair in range(PAIRS)]:
        finish(*item)
    core = core_ref[0]
    targets = [(1 - core, send_hbm), (core, keep_hbm)]
    back[:, WIDTH:] = ctx[...]
    for start in range(0, WIDTH, BLOCK):
        columns = slice(start, start + BLOCK)
        back[:, columns] = dot_nt(grads[...], w_qkv[columns]).astype(BF)
    weight_terms(x, c, grads, ctx, terms, targets, sems, [(back, back_hbm)])


def wait_all(copies):
    for copy in copies:
        copy.wait()


def start_all(copies):
    for copy in copies:
        copy.start()
    return copies


def weight_copies(qkv_hbm, w_qkv, sems, first):
    return [
        pltpu.make_async_copy(
            qkv_hbm.at[:, pl.ds(part * WIDTH + first, HALF_WIDTH)], w_qkv.at[part], sems.at[part]
        )
        for part in range(3)
    ]


def grads_times_weights(grads, w_qkv, columns):
    return sum(
        dot_nt(grads[:, part * HALF_WIDTH : (part + 1) * HALF_WIDTH], w_qkv[part, columns]) for part in range(3)
    )


def final_kernel(
    grads_hbm, ctx_hbm, back_hbm, qkv_hbm, out_hbm, attention_hbm, normed_hbm,
    grads, ctx, back, w_qkv, w_out, attention, normed, sems, out_sems,
):
    ins = start_all(
        [
            pltpu.make_async_copy(source, target, sems.at[3 + index])
            for index, (source, target) in enumerate(
                ((ctx_hbm, ctx), (back_hbm, back), (out_hbm, w_out), (grads_hbm, grads))
            )
        ]
        + weight_copies(qkv_hbm, w_qkv, sems, 0)
    )
    outs = []
    wait_all(ins[:3])
    for index in range(3):
        columns = slice(index * BLOCK, (index + 1) * BLOCK)
        span = pl.ds(index * BLOCK, BLOCK)
        attention[:, columns] = (
            dot_nt(ctx[...], w_out[columns, :HALF_WIDTH]) + dot_nt(back[:, WIDTH:], w_out[columns, HALF_WIDTH:])
        ).astype(BF)
        outs += start_all(
            [pltpu.make_async_copy(attention.at[:, span], attention_hbm.at[:, span], out_sems.at[0, index])]
        )
    wait_all(ins[3:])
    for index in range(3):
        columns = slice(index * BLOCK, (index + 1) * BLOCK)
        span = pl.ds(index * BLOCK, BLOCK)
        normed[:, columns] = (
            back[:, columns].astype(F32) + grads_times_weights(grads, w_qkv, columns)
        ).astype(BF)
        outs += start_all([pltpu.make_async_copy(normed.at[:, span], normed_hbm.at[:, span], out_sems.at[1, index])])
    wait_all(outs)


def order_kernel(back_hbm, first, second, third, out_hbm, zeros, sems):
    zeros[...] = jnp.zeros_like(zeros)
    wait_all(start_all([pltpu.make_async_copy(zeros, out_hbm, sems.at[0])]))


def pack_kernel(x_hbm, c_hbm, both_hbm, both, sems, out_sems):
    spans = [pl.ds(2 * index, 2) for index in range(4)]
    ins = start_all(
        [
            pltpu.make_async_copy(source.at[span], both.at[span, place], sems.at[place, index])
            for index, span in enumerate(spans)
            for place, source in enumerate((x_hbm, c_hbm))
        ]
    )
    outs = []
    for index, span in enumerate(spans):
        wait_all(ins[2 * index : 2 * index + 2])
        outs += start_all([pltpu.make_async_copy(both.at[span], both_hbm.at[span], out_sems.at[index])])
    wait_all(outs)


def pair_sum_kernel(x_ref, keep_hbm, received_hbm, *refs):
    out_hbms = refs[-8:-4]
    terms, totals, sems, out_sems = refs[-4:]
    ins, outs = [], []
    order = (1, 3, 2, 0)
    for step in order:
        place = pl.ds(2 * lax.rem(x_ref[0] + step, 4), 2)
        for index, source in enumerate((keep_hbm, received_hbm)):
            ins += start_all(
                [pltpu.make_async_copy(source.at[place], terms.at[step, index], sems.at[index, step])]
            )
    for index, step in enumerate(order):
        wait_all(ins[2 * index : 2 * index + 2])
        totals[step] = (terms[step, 0].astype(F32) + terms[step, 1].astype(F32)).astype(BF)
        outs += start_all([pltpu.make_async_copy(totals.at[step], out_hbms[step], out_sems.at[step])])
    wait_all(outs)


def ring_sum_kernel(*refs):
    in_hbms, (out_hbm, terms, totals, sems, out_sems) = refs[:8], refs[9:]
    ins = [
        start_all(
            [
                pltpu.make_async_copy(source.at[z_hi], terms.at[index, z_hi], sems.at[index, z_hi])
                for index, source in enumerate(in_hbms)
            ]
        )
        for z_hi in range(2)
    ]
    outs = []
    for z_hi in range(2):
        wait_all(ins[z_hi])
        for half in range(2):
            total = sum(terms[4 * half + step, z_hi].astype(F32) for step in range(4))
            for z_lo in range(2):
                totals[z_hi, :, z_lo, half] = total[:, 24 * z_lo : 24 * z_lo + 24].astype(BF)
        outs += start_all([pltpu.make_async_copy(totals.at[z_hi], out_hbm.at[z_hi], out_sems.at[z_hi])])
    wait_all(outs)


def group_sum_kernel(pieces_hbm, after, out_hbm, pieces, total, sems, in_sems):
    ins = start_all(
        [
            pltpu.make_async_copy(pieces_hbm.at[pl.ds(4 * index, 4)], pieces.at[pl.ds(4 * index, 4)], in_sems.at[index])
            for index in range(4)
        ]
    )
    parts = []
    for index in range(4):
        ins[index].wait()
        parts.append(jnp.sum(pieces[4 * index : 4 * index + 4].astype(F32), axis=0))
    total[...] = sum(parts).astype(BF)
    wait_all(
        start_all([pltpu.make_async_copy(total, out_hbm.at[place], sems.at[place]) for place in range(8)])
    )


def assemble_kernel(factor, whole, qkv_hbm, out_hbm, qkv_grad, out_grad, sems):
    outs = []
    for z_lo in range(2):
        rows, span = slice(24 * z_lo, 24 * z_lo + 24), pl.ds(24 * z_lo, 24)
        for part in range(4):
            for half in range(2):
                value = whole[4 * z_lo + part, half].astype(F32) * factor
                start = half * HALF_WIDTH
                if part < 3:
                    start += part * WIDTH
                    qkv_grad[rows, start : start + HALF_WIDTH] = value
                else:
                    out_grad[rows, start : start + HALF_WIDTH] = value
        outs += start_all(
            [
                pltpu.make_async_copy(qkv_grad.at[span], qkv_hbm.at[span], sems.at[0, z_lo]),
                pltpu.make_async_copy(out_grad.at[span], out_hbm.at[span], sems.at[1, z_lo]),
            ]
        )
    wait_all(outs)


SMEM = pl.BlockSpec(memory_space=pltpu.SMEM)
HBM = pl.BlockSpec(memory_space=pltpu.HBM)


def buffer(*dims, dtype=BF):
    return pltpu.VMEM(dims, dtype)


def copy_sems(*dims):
    return pltpu.SemaphoreType.DMA(dims)


def shape(*dims, dtype=BF):
    return jax.ShapeDtypeStruct(dims, dtype)


def call(kernel, out_shape, flops, scratch, arrays, mib=64, held=None):
    scalars = sum(1 for array in arrays if array.ndim == 1)
    return pl.pallas_call(
        kernel,
        out_shape=out_shape,
        in_specs=[SMEM] * scalars + [held or HBM] * (len(arrays) - scalars),
        out_specs=jax.tree.map(lambda _: HBM, out_shape),
        scratch_shapes=scratch,
        compiler_params=pltpu.CompilerParams(vmem_limit_bytes=mib * MIB),
        cost_estimate=pl.CostEstimate(flops=flops, bytes_accessed=2 ** 16, transcendentals=0),
    )(*arrays)


def sublayer(kernel, dims, out_shapes, scratch, *arrays):
    return call(
        kernel,
        (*out_shapes, shape(ROWS, 4, 48, HALF_WIDTH), shape(ROWS, 4, 48, HALF_WIDTH)),
        2 * 10 ** 10,
        [
            buffer(*dims),
            buffer(*dims),
            buffer(WIDTH, 3 * HALF_WIDTH),
            buffer(WIDTH, HALF_WIDTH),
            buffer(POSITIONS, 3 * HALF_WIDTH),
            buffer(POSITIONS, HALF_WIDTH),
            buffer(POSITIONS, 3 * HALF_WIDTH),
            buffer(POSITIONS, HALF_WIDTH),
            buffer(ROWS, 2, 4, 48, HALF_WIDTH),
            copy_sems(10),
            *scratch,
        ],
        arrays,
        mib=64,
    )


def swap(part, axis, groups=None):
    return lax.all_to_all(part, axis, split_axis=0, concat_axis=0, tiled=True, axis_index_groups=groups)


def plane_groups():
    def flat(x, z_hi, core, z_lo, y):
        return ((x * 2 + z_hi) * 2 + core) * 8 + z_lo * 4 + y

    return [
        [flat(x, z_hi, core, z_lo, y) for z_hi in range(2) for y in range(4) for z_lo in range(2)]
        for x in range(4)
        for core in range(2)
    ]


def exchange(send):
    return lax.ppermute(send, "dp", [(i, i ^ 1) for i in range(16)])


def pair_sum(x_index, keep, send, *after):
    return call(
        pair_sum_kernel,
        (shape(2, 4, 48, HALF_WIDTH),) * 4,
        2 * 10 ** 9,
        [buffer(4, 2, 2, 4, 48, HALF_WIDTH), buffer(4, 2, 4, 48, HALF_WIDTH), copy_sems(2, 4), copy_sems(4)],
        (x_index, keep, exchange(send), *after),
    )


def ring(parts):
    return [parts[0]] + [
        lax.ppermute(parts[step], "dp", [(i, (i + 4 * step) % 16) for i in range(16)]) for step in range(1, 4)
    ]


def body(normed, cotangent, qkv_weight, out_weight):
    x, c = normed[0], cotangent[0]
    dp = lax.axis_index("dp")
    core = (dp % 2).reshape(1)
    x_index = (dp // 4).reshape(1)
    grid_dims = (ROWS, COLUMNS, WIDTH)
    both = call(
        pack_kernel,
        shape(ROWS, 2, COLUMNS, WIDTH),
        10 ** 6,
        [buffer(ROWS, 2, COLUMNS, WIDTH), copy_sems(2, 4), copy_sems(4)],
        (x.reshape(grid_dims), c.reshape(grid_dims)),
    )
    both = swap(both, "ctx")
    grads_row, ctx_row, keep_row, send_row = sublayer(
        row_kernel,
        (POSITIONS, WIDTH),
        [shape(POSITIONS, 3 * HALF_WIDTH), shape(POSITIONS, HALF_WIDTH)],
        [buffer(PAIRS, 2, POSITIONS, POSITIONS)] * 2,
        core, x, c, qkv_weight, out_weight,
    )
    terms_row = ring(pair_sum(x_index, keep_row, send_row))
    back_width = WIDTH + HALF_WIDTH
    back, keep_col, send_col = sublayer(
        column_kernel,
        grid_dims,
        [shape(POSITIONS, back_width)],
        [buffer(POSITIONS, back_width)],
        core, both, qkv_weight, out_weight, terms_row[0],
    )
    order = call(order_kernel, shape(8, PAIR, dtype=F32), 4 * 10 ** 10, [buffer(8, PAIR, dtype=F32), copy_sems(1)], (back, *terms_row[1:]))
    parts = pair_sum(x_index, keep_col, send_col, order)
    terms_col = ring(parts)
    back = swap(back.reshape(ROWS, COLUMNS, back_width), "ctx").reshape(POSITIONS, back_width)
    attention_out, normed_grad = call(
        final_kernel,
        (shape(POSITIONS, WIDTH),) * 2,
        4 * 10 ** 9,
        [
            buffer(POSITIONS, 3 * HALF_WIDTH),
            buffer(POSITIONS, HALF_WIDTH),
            buffer(POSITIONS, back_width),
            buffer(3, WIDTH, HALF_WIDTH),
            buffer(WIDTH, WIDTH),
            buffer(POSITIONS, WIDTH),
            buffer(POSITIONS, WIDTH),
            copy_sems(7),
            copy_sems(2, 4),
        ],
        (grads_row, ctx_row, back, qkv_weight, out_weight),
        mib=64,
    )
    terms = call(
        ring_sum_kernel,
        shape(2, 4, 2, 2, 24, HALF_WIDTH),
        2 * 10 ** 9,
        [buffer(8, 2, 4, 48, HALF_WIDTH), buffer(2, 4, 2, 2, 24, HALF_WIDTH), copy_sems(8, 2), copy_sems(2)],
        (*terms_row, *terms_col, back),
    )
    pieces = swap(terms.reshape(16, 2, 24, HALF_WIDTH), ("dp", "ctx"), plane_groups())
    own = call(
        group_sum_kernel,
        shape(8, 2, 24, HALF_WIDTH),
        10 ** 9,
        [buffer(16, 2, 24, HALF_WIDTH), buffer(2, 24, HALF_WIDTH), copy_sems(8), copy_sems(4)],
        (pieces, attention_out),
    )
    whole = swap(own, "ctx")
    factor = (lax.axis_size("dp") * lax.axis_size("ctx") * POSITIONS) ** (-0.5)
    qkv_grad, out_grad = call(
        functools.partial(assemble_kernel, factor),
        (shape(48, 3 * WIDTH, dtype=F32), shape(48, WIDTH, dtype=F32)),
        10 ** 6,
        [
            buffer(48, 3 * WIDTH, dtype=F32),
            buffer(48, WIDTH, dtype=F32),
            copy_sems(2, 2),
        ],
        (whole,),
        mib=8,
        held=pl.BlockSpec(memory_space=pltpu.VMEM),
    )
    return (attention_out[None], normed_grad[None], qkv_grad, out_grad)


def solution(mesh):
    placed = (P("dp", "ctx", None), P("dp", "ctx", None), P(), P())
    return jax.shard_map(
        body,
        mesh=mesh,
        in_specs=placed,
        out_specs=(P("dp", "ctx", None), P("dp", "ctx", None), P("dp", None), P("dp", None)),
        check_vma=False,
    )
```

```python
import functools

import jax
import jax.numpy as jnp
from jax import lax
from jax.experimental import pallas as pl
from jax.experimental.pallas import tpu as pltpu
from jax.sharding import PartitionSpec as P

WIDTH = 768
HALF_WIDTH = 384
HEAD_DIM = 64
POSITIONS = 512
ROWS = 8
COLUMNS = 64
PAIR = 128
PAIRS = HALF_WIDTH // PAIR
BLOCK = 256
CHUNK = 16
BF = jnp.bfloat16
F32 = jnp.float32
MIB = 1024 * 1024


def dot(a, b):
    return lax.dot_general(a, b, (((1,), (0,)), ((), ())), preferred_element_type=F32)


def dot_nt(a, b):
    return lax.dot_general(a, b, (((1,), (1,)), ((), ())), preferred_element_type=F32)


def dot_tn(a, b):
    return lax.dot_general(a, b, (((0,), (0,)), ((), ())), preferred_element_type=F32)


def half_lanes(array, half):
    lane = lax.broadcasted_iota(jnp.int32, array.shape, array.ndim - 1)
    inside = (lane >= HEAD_DIM) if half else (lane < HEAD_DIM)
    return jnp.where(inside, array, jnp.zeros_like(array))


def probabilities(scores, start):
    square = scores[:, start:]
    row = lax.broadcasted_iota(jnp.int32, square.shape, 0)
    square = jnp.where(lax.broadcasted_iota(jnp.int32, square.shape, 1) <= row, square, -1e30)
    scores = jnp.concatenate([scores[:, :start], square], axis=1) if start else square
    top = jnp.max(scores, axis=-1, keepdims=True)
    weights = jnp.exp(scores - top)
    return weights * (1.0 / jnp.sum(weights, axis=-1, keepdims=True))


def chunk_probabilities(scores, allowed):
    scores = jnp.where(allowed, scores, -1e30)
    top = jnp.max(scores, axis=-1, keepdims=True)
    weights = jnp.exp(scores - top)
    return weights * (1.0 / jnp.sum(weights, axis=-1, keepdims=True))


def load(x_hbm, c_hbm, qkv_hbm, out_hbm, x, c, w_qkv, w_out, sems, first):
    copies = [pltpu.make_async_copy(x_hbm, x, sems.at[0])]
    for part in range(3):
        columns = pl.ds(part * WIDTH + first, HALF_WIDTH)
        place = pl.ds(part * HALF_WIDTH, HALF_WIDTH)
        copies.append(pltpu.make_async_copy(qkv_hbm.at[:, columns], w_qkv.at[:, place], sems.at[1 + part]))
    copies.append(pltpu.make_async_copy(c_hbm, c, sems.at[4]))
    copies.append(pltpu.make_async_copy(out_hbm.at[:, pl.ds(first, HALF_WIDTH)], w_out, sems.at[5]))
    for copy in copies:
        copy.start()
    return copies


def project(copies, x, c, w_qkv, w_out, proj, gctx):
    copies[0].wait()
    for part in range(3):
        copies[1 + part].wait()
        columns = slice(part * HALF_WIDTH, (part + 1) * HALF_WIDTH)
        piece = dot(x[...].reshape(POSITIONS, WIDTH), w_qkv[:, columns]).astype(BF)
        if part == 0:
            piece = piece * BF(HEAD_DIM ** -0.5)
        proj[:, columns] = piece
    copies[4].wait()
    copies[5].wait()
    gctx[...] = dot(c[...].reshape(POSITIONS, WIDTH), w_out[...]).astype(BF)


def weight_terms(x, c, grads, ctx, terms, targets, sems, extra):
    copies = []
    for part in range(4):
        for index, (place, target) in enumerate(targets):
            copies.append(
                pltpu.make_async_copy(terms.at[:, place, part], target.at[:, part], sems.at[2 + 4 * index + part])
            )
    extra = start_all(
        [pltpu.make_async_copy(source, target, sems.at[index]) for index, (source, target) in enumerate(extra)]
    )
    x_t = jnp.transpose(x[...].reshape(POSITIONS, WIDTH))
    for part in range(3):
        res = dot(x_t, grads[:, part * HALF_WIDTH : (part + 1) * HALF_WIDTH]).astype(BF)
        terms[:, :, part] = res.reshape(ROWS, 2, 48, HALF_WIDTH)
        copies[2 * part].start()
        copies[2 * part + 1].start()
    c_t = jnp.transpose(c[...].reshape(POSITIONS, WIDTH))
    terms[:, :, 3] = dot(c_t, ctx[...]).astype(BF).reshape(ROWS, 2, 48, HALF_WIDTH)
    copies[6].start()
    copies[7].start()
    wait_all(extra + copies)


def row_kernel(
    core_ref, x_hbm, c_hbm, qkv_hbm, out_hbm, grads_hbm, ctx_hbm, keep_hbm, send_hbm,
    x, c, w_qkv, w_out, proj, gctx, grads, ctx, terms, sems, probs, dscores,
):
    copies = load(x_hbm, c_hbm, qkv_hbm, out_hbm, x, c, w_qkv, w_out, sems, 0)
    project(copies, x, c, w_qkv, w_out, proj, gctx)
    def products(pair, start):
        lanes = slice(pair * PAIR, (pair + 1) * PAIR)
        stop = start + BLOCK
        query, grad = proj[start:stop, lanes], gctx[start:stop, lanes]
        keys = [half_lanes(proj[:stop, HALF_WIDTH + pair * PAIR : HALF_WIDTH + (pair + 1) * PAIR], h) for h in range(2)]
        values = [
            half_lanes(proj[:stop, 2 * HALF_WIDTH + pair * PAIR : 2 * HALF_WIDTH + (pair + 1) * PAIR], h)
            for h in range(2)
        ]
        scores = [dot_nt(query, key) for key in keys]
        return pair, start, keys, values, scores, [dot_nt(grad, value) for value in values]

    def softmax(pair, start, keys, values, scores, grad_weights):
        lanes = slice(pair * PAIR, (pair + 1) * PAIR)
        stop = start + BLOCK
        outs, dqs = [], []
        weights = [probabilities(scores[half], start) for half in range(2)]
        for half in range(2):
            rounded = weights[half].astype(BF)
            probs[pair, half, start:stop, :stop] = rounded
            outs.append(dot(rounded, values[half]))
            delta = jnp.sum(weights[half] * grad_weights[half], axis=-1, keepdims=True)
            ds = (weights[half] * (grad_weights[half] - delta)).astype(BF)
            dscores[pair, half, start:stop, :stop] = ds
            dqs.append(dot(ds, keys[half]))
        ctx[start:stop, lanes] = (outs[0] + outs[1]).astype(BF)
        grads[start:stop, lanes] = ((dqs[0] + dqs[1]) * (HEAD_DIM ** -0.5)).astype(BF)

    def key_sums(pair):
        lanes = slice(pair * PAIR, (pair + 1) * PAIR)
        k_lanes = slice(HALF_WIDTH + pair * PAIR, HALF_WIDTH + (pair + 1) * PAIR)
        v_lanes = slice(2 * HALF_WIDTH + pair * PAIR, 2 * HALF_WIDTH + (pair + 1) * PAIR)
        query_t = jnp.transpose(proj[:, lanes])
        grad_t = jnp.transpose(gctx[:, lanes])
        for start in range(0, POSITIONS, BLOCK):
            stop = start + BLOCK
            for place, left, right in ((k_lanes, query_t, dscores), (v_lanes, grad_t, probs)):
                both = jnp.concatenate(
                    [
                        dot(left[half * HEAD_DIM : (half + 1) * HEAD_DIM, start:], right[pair, half, start:, start:stop])
                        for half in range(2)
                    ],
                    axis=0,
                )
                grads[start:stop, place] = jnp.transpose(both.astype(BF))

    order = [(pair, start) for pair in range(PAIRS) for start in range(0, POSITIONS, BLOCK)]
    held = products(*order[0])
    for index, (pair, start) in enumerate(order):
        following = products(*order[index + 1]) if index + 1 < len(order) else None
        softmax(*held)
        held = following
        if start and pair:
            key_sums(pair - 1)
    key_sums(PAIRS - 1)
    core = core_ref[0]
    targets = [(1 - core, send_hbm), (core, keep_hbm)]
    weight_terms(x, c, grads, ctx, terms, targets, sems, [(grads, grads_hbm), (ctx, ctx_hbm)])


def column_kernel(
    core_ref, both_hbm, qkv_hbm, out_hbm, after, back_hbm, keep_hbm, send_hbm,
    x, c, w_qkv, w_out, proj, gctx, grads, ctx, terms, sems, back,
):
    x_hbm, c_hbm = both_hbm.at[:, 0], both_hbm.at[:, 1]
    copies = load(x_hbm, c_hbm, qkv_hbm, out_hbm, x, c, w_qkv, w_out, sems, HALF_WIDTH)
    project(copies, x, c, w_qkv, w_out, proj, gctx)
    size = ROWS * CHUNK
    chunks = COLUMNS // CHUNK
    line = lax.broadcasted_iota(jnp.int32, (size, size), 0)
    across = lax.broadcasted_iota(jnp.int32, (size, size), 1)
    allowed = ((line % CHUNK) == (across % CHUNK)) & (across <= line)
    allowed = jnp.concatenate([allowed.astype(F32)] * chunks, axis=0) > 0

    def twice(array):
        return jnp.concatenate([half_lanes(array, 0), half_lanes(array, 1)], axis=0)

    def gather(ref, base):
        whole = ref[:, base : base + PAIR].reshape(ROWS, COLUMNS, PAIR)
        return [
            whole[:, t * CHUNK : (t + 1) * CHUNK].reshape(size, PAIR) for t in range(chunks)
        ]

    def scatter(ref, base, pieces):
        whole = jnp.concatenate([p.reshape(ROWS, CHUNK, PAIR) for p in pieces], axis=1)
        ref[:, base : base + PAIR] = whole.reshape(POSITIONS, PAIR)

    def products(pair):
        base = pair * PAIR
        query, key, value = [gather(proj, part * HALF_WIDTH + base) for part in range(3)]
        grad = gather(gctx, base)
        keys, values, queries, grad_parts = [[twice(t) for t in part] for part in (key, value, query, grad)]
        scores = jnp.concatenate([dot_nt(a, b) for a, b in zip(query, keys)], axis=0)
        grad_weights = jnp.concatenate([dot_nt(a, b) for a, b in zip(grad, values)], axis=0)
        return base, keys, values, queries, grad_parts, scores, grad_weights

    def finish(base, keys, values, queries, grad_parts, scores, grad_weights):
        rounded, dscores = [], []
        for half in range(2):
            lanes = slice(half * size, (half + 1) * size)
            weights = chunk_probabilities(scores[:, lanes], allowed)
            rounded.append(weights.astype(BF))
            part = grad_weights[:, lanes]
            delta = jnp.sum(weights * part, axis=-1, keepdims=True)
            dscores.append((weights * (part - delta)).astype(BF))
        outs, dqs, dks, dvs = [], [], [], []
        for t in range(chunks):
            rows = slice(t * size, (t + 1) * size)
            wide = [jnp.concatenate([pieces[0][rows], pieces[1][rows]], axis=1) for pieces in (rounded, dscores)]
            tall = [jnp.concatenate([pieces[0][rows], pieces[1][rows]], axis=0) for pieces in (rounded, dscores)]
            outs.append(dot(wide[0], values[t]).astype(BF))
            dqs.append((dot(wide[1], keys[t]) * (HEAD_DIM ** -0.5)).astype(BF))
            dks.append(dot_tn(tall[1], queries[t]).astype(BF))
            dvs.append(dot_tn(tall[0], grad_parts[t]).astype(BF))
        scatter(ctx, base, outs)
        scatter(grads, base, dqs)
        scatter(grads, HALF_WIDTH + base, dks)
        scatter(grads, 2 * HALF_WIDTH + base, dvs)

    for item in [products(pair) for pair in range(PAIRS)]:
        finish(*item)
    core = core_ref[0]
    targets = [(1 - core, send_hbm), (core, keep_hbm)]
    back[:, WIDTH:] = ctx[...]
    for start in range(0, WIDTH, BLOCK):
        columns = slice(start, start + BLOCK)
        back[:, columns] = dot_nt(grads[...], w_qkv[columns]).astype(BF)
    weight_terms(x, c, grads, ctx, terms, targets, sems, [(back, back_hbm)])


def wait_all(copies):
    for copy in copies:
        copy.wait()


def start_all(copies):
    for copy in copies:
        copy.start()
    return copies


def weight_copies(qkv_hbm, w_qkv, sems, first):
    return [
        pltpu.make_async_copy(
            qkv_hbm.at[:, pl.ds(part * WIDTH + first, HALF_WIDTH)], w_qkv.at[part], sems.at[part]
        )
        for part in range(3)
    ]


def grads_times_weights(grads, w_qkv, columns):
    return sum(
        dot_nt(grads[:, part * HALF_WIDTH : (part + 1) * HALF_WIDTH], w_qkv[part, columns]) for part in range(3)
    )


def final_kernel(
    grads_hbm, ctx_hbm, back_hbm, qkv_hbm, out_hbm, attention_hbm, normed_hbm,
    grads, ctx, back, w_qkv, w_out, attention, normed, sems, out_sems,
):
    ins = start_all(
        [
            pltpu.make_async_copy(source, target, sems.at[3 + index])
            for index, (source, target) in enumerate(
                ((ctx_hbm, ctx), (back_hbm, back), (out_hbm, w_out), (grads_hbm, grads))
            )
        ]
        + weight_copies(qkv_hbm, w_qkv, sems, 0)
    )
    outs = []
    wait_all(ins[:3])
    for index in range(3):
        columns = slice(index * BLOCK, (index + 1) * BLOCK)
        span = pl.ds(index * BLOCK, BLOCK)
        attention[:, columns] = (
            dot_nt(ctx[...], w_out[columns, :HALF_WIDTH]) + dot_nt(back[:, WIDTH:], w_out[columns, HALF_WIDTH:])
        ).astype(BF)
        outs += start_all(
            [pltpu.make_async_copy(attention.at[:, span], attention_hbm.at[:, span], out_sems.at[0, index])]
        )
    wait_all(ins[3:])
    for index in range(3):
        columns = slice(index * BLOCK, (index + 1) * BLOCK)
        span = pl.ds(index * BLOCK, BLOCK)
        normed[:, columns] = (
            back[:, columns].astype(F32) + grads_times_weights(grads, w_qkv, columns)
        ).astype(BF)
        outs += start_all([pltpu.make_async_copy(normed.at[:, span], normed_hbm.at[:, span], out_sems.at[1, index])])
    wait_all(outs)


def order_kernel(back_hbm, first, second, third, out_hbm, zeros, sems):
    zeros[...] = jnp.zeros_like(zeros)
    wait_all(start_all([pltpu.make_async_copy(zeros, out_hbm, sems.at[0])]))


def pack_kernel(x_hbm, c_hbm, both_hbm, both, sems, out_sems):
    spans = [pl.ds(2 * index, 2) for index in range(4)]
    ins = start_all(
        [
            pltpu.make_async_copy(source.at[span], both.at[span, place], sems.at[place, index])
            for index, span in enumerate(spans)
            for place, source in enumerate((x_hbm, c_hbm))
        ]
    )
    outs = []
    for index, span in enumerate(spans):
        wait_all(ins[2 * index : 2 * index + 2])
        outs += start_all([pltpu.make_async_copy(both.at[span], both_hbm.at[span], out_sems.at[index])])
    wait_all(outs)


def pair_sum_kernel(x_ref, keep_hbm, received_hbm, *refs):
    out_hbms = refs[-8:-4]
    terms, totals, sems, out_sems = refs[-4:]
    ins, outs = [], []
    order = (1, 3, 2, 0)
    for step in order:
        place = pl.ds(2 * lax.rem(x_ref[0] + step, 4), 2)
        for index, source in enumerate((keep_hbm, received_hbm)):
            ins += start_all(
                [pltpu.make_async_copy(source.at[place], terms.at[step, index], sems.at[index, step])]
            )
    for index, step in enumerate(order):
        wait_all(ins[2 * index : 2 * index + 2])
        totals[step] = (terms[step, 0].astype(F32) + terms[step, 1].astype(F32)).astype(BF)
        outs += start_all([pltpu.make_async_copy(totals.at[step], out_hbms[step], out_sems.at[step])])
    wait_all(outs)


def ring_sum_kernel(*refs):
    in_hbms, (out_hbm, terms, totals, sems, out_sems) = refs[:8], refs[9:]
    ins = [
        start_all(
            [
                pltpu.make_async_copy(source.at[z_hi], terms.at[index, z_hi], sems.at[index, z_hi])
                for index, source in enumerate(in_hbms)
            ]
        )
        for z_hi in range(2)
    ]
    outs = []
    for z_hi in range(2):
        wait_all(ins[z_hi])
        for half in range(2):
            total = sum(terms[4 * half + step, z_hi].astype(F32) for step in range(4))
            for z_lo in range(2):
                totals[z_hi, :, z_lo, half] = total[:, 24 * z_lo : 24 * z_lo + 24].astype(BF)
        outs += start_all([pltpu.make_async_copy(totals.at[z_hi], out_hbm.at[z_hi], out_sems.at[z_hi])])
    wait_all(outs)


def group_sum_kernel(pieces_hbm, after, out_hbm, pieces, total, sems, in_sems):
    ins = start_all(
        [
            pltpu.make_async_copy(pieces_hbm.at[pl.ds(4 * index, 4)], pieces.at[pl.ds(4 * index, 4)], in_sems.at[index])
            for index in range(4)
        ]
    )
    parts = []
    for index in range(4):
        ins[index].wait()
        parts.append(jnp.sum(pieces[4 * index : 4 * index + 4].astype(F32), axis=0))
    total[...] = sum(parts).astype(BF)
    wait_all(
        start_all([pltpu.make_async_copy(total, out_hbm.at[place], sems.at[place]) for place in range(8)])
    )


def assemble_kernel(factor, whole, qkv_hbm, out_hbm, qkv_grad, out_grad, sems):
    outs = []
    for z_lo in range(2):
        rows, span = slice(24 * z_lo, 24 * z_lo + 24), pl.ds(24 * z_lo, 24)
        for part in range(4):
            for half in range(2):
                value = whole[4 * z_lo + part, half].astype(F32) * factor
                start = half * HALF_WIDTH
                if part < 3:
                    start += part * WIDTH
                    qkv_grad[rows, start : start + HALF_WIDTH] = value
                else:
                    out_grad[rows, start : start + HALF_WIDTH] = value
        outs += start_all(
            [
                pltpu.make_async_copy(qkv_grad.at[span], qkv_hbm.at[span], sems.at[0, z_lo]),
                pltpu.make_async_copy(out_grad.at[span], out_hbm.at[span], sems.at[1, z_lo]),
            ]
        )
    wait_all(outs)


SMEM = pl.BlockSpec(memory_space=pltpu.SMEM)
HBM = pl.BlockSpec(memory_space=pltpu.HBM)


def buffer(*dims, dtype=BF):
    return pltpu.VMEM(dims, dtype)


def copy_sems(*dims):
    return pltpu.SemaphoreType.DMA(dims)


def shape(*dims, dtype=BF):
    return jax.ShapeDtypeStruct(dims, dtype)


def call(kernel, out_shape, flops, scratch, arrays, mib=64, held=None):
    scalars = sum(1 for array in arrays if array.ndim == 1)
    return pl.pallas_call(
        kernel,
        out_shape=out_shape,
        in_specs=[SMEM] * scalars + [held or HBM] * (len(arrays) - scalars),
        out_specs=jax.tree.map(lambda _: HBM, out_shape),
        scratch_shapes=scratch,
        compiler_params=pltpu.CompilerParams(vmem_limit_bytes=mib * MIB),
        cost_estimate=pl.CostEstimate(flops=flops, bytes_accessed=2 ** 16, transcendentals=0),
    )(*arrays)


def sublayer(kernel, dims, out_shapes, scratch, *arrays):
    return call(
        kernel,
        (*out_shapes, shape(ROWS, 4, 48, HALF_WIDTH), shape(ROWS, 4, 48, HALF_WIDTH)),
        2 * 10 ** 10,
        [
            buffer(*dims),
            buffer(*dims),
            buffer(WIDTH, 3 * HALF_WIDTH),
            buffer(WIDTH, HALF_WIDTH),
            buffer(POSITIONS, 3 * HALF_WIDTH),
            buffer(POSITIONS, HALF_WIDTH),
            buffer(POSITIONS, 3 * HALF_WIDTH),
            buffer(POSITIONS, HALF_WIDTH),
            buffer(ROWS, 2, 4, 48, HALF_WIDTH),
            copy_sems(10),
            *scratch,
        ],
        arrays,
        mib=64,
    )


def swap(part, axis, groups=None):
    return lax.all_to_all(part, axis, split_axis=0, concat_axis=0, tiled=True, axis_index_groups=groups)


def plane_groups():
    def flat(x, z_hi, core, z_lo, y):
        return ((x * 2 + z_hi) * 2 + core) * 8 + z_lo * 4 + y

    return [
        [flat(x, z_hi, core, z_lo, y) for z_hi in range(2) for y in range(4) for z_lo in range(2)]
        for x in range(4)
        for core in range(2)
    ]


def exchange(send):
    return lax.ppermute(send, "dp", [(i, i ^ 1) for i in range(16)])


def pair_sum(x_index, keep, send, *after):
    return call(
        pair_sum_kernel,
        (shape(2, 4, 48, HALF_WIDTH),) * 4,
        2 * 10 ** 9,
        [buffer(4, 2, 2, 4, 48, HALF_WIDTH), buffer(4, 2, 4, 48, HALF_WIDTH), copy_sems(2, 4), copy_sems(4)],
        (x_index, keep, exchange(send), *after),
    )


def ring(parts):
    return [parts[0]] + [
        lax.ppermute(parts[step], "dp", [(i, (i + 4 * step) % 16) for i in range(16)]) for step in (2, 3, 1)
    ]


def body(normed, cotangent, qkv_weight, out_weight):
    x, c = normed[0], cotangent[0]
    dp = lax.axis_index("dp")
    core = (dp % 2).reshape(1)
    x_index = (dp // 4).reshape(1)
    grid_dims = (ROWS, COLUMNS, WIDTH)
    both = call(
        pack_kernel,
        shape(ROWS, 2, COLUMNS, WIDTH),
        10 ** 6,
        [buffer(ROWS, 2, COLUMNS, WIDTH), copy_sems(2, 4), copy_sems(4)],
        (x.reshape(grid_dims), c.reshape(grid_dims)),
    )
    both = swap(both, "ctx")
    grads_row, ctx_row, keep_row, send_row = sublayer(
        row_kernel,
        (POSITIONS, WIDTH),
        [shape(POSITIONS, 3 * HALF_WIDTH), shape(POSITIONS, HALF_WIDTH)],
        [buffer(PAIRS, 2, POSITIONS, POSITIONS)] * 2,
        core, x, c, qkv_weight, out_weight,
    )
    terms_row = ring(pair_sum(x_index, keep_row, send_row))
    back_width = WIDTH + HALF_WIDTH
    back, keep_col, send_col = sublayer(
        column_kernel,
        grid_dims,
        [shape(POSITIONS, back_width)],
        [buffer(POSITIONS, back_width)],
        core, both, qkv_weight, out_weight, terms_row[0],
    )
    order = call(order_kernel, shape(8, PAIR, dtype=F32), 4 * 10 ** 10, [buffer(8, PAIR, dtype=F32), copy_sems(1)], (back, *terms_row[1:]))
    parts = pair_sum(x_index, keep_col, send_col, order)
    terms_col = ring(parts)
    back = swap(back.reshape(ROWS, COLUMNS, back_width), "ctx").reshape(POSITIONS, back_width)
    attention_out, normed_grad = call(
        final_kernel,
        (shape(POSITIONS, WIDTH),) * 2,
        4 * 10 ** 9,
        [
            buffer(POSITIONS, 3 * HALF_WIDTH),
            buffer(POSITIONS, HALF_WIDTH),
            buffer(POSITIONS, back_width),
            buffer(3, WIDTH, HALF_WIDTH),
            buffer(WIDTH, WIDTH),
            buffer(POSITIONS, WIDTH),
            buffer(POSITIONS, WIDTH),
            copy_sems(7),
            copy_sems(2, 4),
        ],
        (grads_row, ctx_row, back, qkv_weight, out_weight),
        mib=64,
    )
    terms = call(
        ring_sum_kernel,
        shape(2, 4, 2, 2, 24, HALF_WIDTH),
        2 * 10 ** 9,
        [buffer(8, 2, 4, 48, HALF_WIDTH), buffer(2, 4, 2, 2, 24, HALF_WIDTH), copy_sems(8, 2), copy_sems(2)],
        (*terms_row, *terms_col, back),
    )
    pieces = swap(terms.reshape(16, 2, 24, HALF_WIDTH), ("dp", "ctx"), plane_groups())
    own = call(
        group_sum_kernel,
        shape(8, 2, 24, HALF_WIDTH),
        10 ** 9,
        [buffer(16, 2, 24, HALF_WIDTH), buffer(2, 24, HALF_WIDTH), copy_sems(8), copy_sems(4)],
        (pieces, attention_out),
    )
    whole = swap(own, "ctx")
    factor = (lax.axis_size("dp") * lax.axis_size("ctx") * POSITIONS) ** (-0.5)
    qkv_grad, out_grad = call(
        functools.partial(assemble_kernel, factor),
        (shape(48, 3 * WIDTH, dtype=F32), shape(48, WIDTH, dtype=F32)),
        10 ** 6,
        [
            buffer(48, 3 * WIDTH, dtype=F32),
            buffer(48, WIDTH, dtype=F32),
            copy_sems(2, 2),
        ],
        (whole,),
        mib=8,
        held=pl.BlockSpec(memory_space=pltpu.VMEM),
    )
    return (attention_out[None], normed_grad[None], qkv_grad, out_grad)


def solution(mesh):
    placed = (P("dp", "ctx", None), P("dp", "ctx", None), P(), P())
    return jax.shard_map(
        body,
        mesh=mesh,
        in_specs=placed,
        out_specs=(P("dp", "ctx", None), P("dp", "ctx", None), P("dp", None), P("dp", None)),
        check_vma=False,
    )
```

```python
import functools

import jax
import jax.numpy as jnp
from jax import lax
from jax.experimental import pallas as pl
from jax.experimental.pallas import tpu as pltpu
from jax.sharding import PartitionSpec as P

WIDTH = 768
HALF_WIDTH = 384
HEAD_DIM = 64
POSITIONS = 512
ROWS = 8
COLUMNS = 64
PAIR = 128
PAIRS = HALF_WIDTH // PAIR
BLOCK = 256
CHUNK = 16
BF = jnp.bfloat16
F32 = jnp.float32
MIB = 1024 * 1024


def dot(a, b):
    return lax.dot_general(a, b, (((1,), (0,)), ((), ())), preferred_element_type=F32)


def dot_nt(a, b):
    return lax.dot_general(a, b, (((1,), (1,)), ((), ())), preferred_element_type=F32)


def dot_tn(a, b):
    return lax.dot_general(a, b, (((0,), (0,)), ((), ())), preferred_element_type=F32)


def half_lanes(array, half):
    lane = lax.broadcasted_iota(jnp.int32, array.shape, array.ndim - 1)
    inside = (lane >= HEAD_DIM) if half else (lane < HEAD_DIM)
    return jnp.where(inside, array, jnp.zeros_like(array))


def probabilities(scores, start):
    square = scores[:, start:]
    row = lax.broadcasted_iota(jnp.int32, square.shape, 0)
    square = jnp.where(lax.broadcasted_iota(jnp.int32, square.shape, 1) <= row, square, -1e30)
    scores = jnp.concatenate([scores[:, :start], square], axis=1) if start else square
    top = jnp.max(scores, axis=-1, keepdims=True)
    weights = jnp.exp(scores - top)
    return weights * (1.0 / jnp.sum(weights, axis=-1, keepdims=True))


def chunk_probabilities(scores, allowed):
    scores = jnp.where(allowed, scores, -1e30)
    top = jnp.max(scores, axis=-1, keepdims=True)
    weights = jnp.exp(scores - top)
    return weights * (1.0 / jnp.sum(weights, axis=-1, keepdims=True))


def load(x_hbm, c_hbm, qkv_hbm, out_hbm, x, c, w_qkv, w_out, sems, first):
    copies = [pltpu.make_async_copy(x_hbm, x, sems.at[0])]
    for part in range(3):
        columns = pl.ds(part * WIDTH + first, HALF_WIDTH)
        place = pl.ds(part * HALF_WIDTH, HALF_WIDTH)
        copies.append(pltpu.make_async_copy(qkv_hbm.at[:, columns], w_qkv.at[:, place], sems.at[1 + part]))
    copies.append(pltpu.make_async_copy(c_hbm, c, sems.at[4]))
    copies.append(pltpu.make_async_copy(out_hbm.at[:, pl.ds(first, HALF_WIDTH)], w_out, sems.at[5]))
    for copy in copies:
        copy.start()
    return copies


def project(copies, x, c, w_qkv, w_out, proj, gctx):
    copies[0].wait()
    for part in range(3):
        copies[1 + part].wait()
        columns = slice(part * HALF_WIDTH, (part + 1) * HALF_WIDTH)
        piece = dot(x[...].reshape(POSITIONS, WIDTH), w_qkv[:, columns]).astype(BF)
        if part == 0:
            piece = piece * BF(HEAD_DIM ** -0.5)
        proj[:, columns] = piece
    copies[4].wait()
    copies[5].wait()
    gctx[...] = dot(c[...].reshape(POSITIONS, WIDTH), w_out[...]).astype(BF)


def weight_terms(x, c, grads, ctx, terms, targets, sems, extra):
    copies = []
    for part in range(4):
        for index, (place, target) in enumerate(targets):
            copies.append(
                pltpu.make_async_copy(terms.at[:, place, part], target.at[:, part], sems.at[2 + 4 * index + part])
            )
    extra = start_all(
        [pltpu.make_async_copy(source, target, sems.at[index]) for index, (source, target) in enumerate(extra)]
    )
    x_t = jnp.transpose(x[...].reshape(POSITIONS, WIDTH))
    for part in range(3):
        res = dot(x_t, grads[:, part * HALF_WIDTH : (part + 1) * HALF_WIDTH]).astype(BF)
        terms[:, :, part] = res.reshape(ROWS, 2, 48, HALF_WIDTH)
        copies[2 * part].start()
        copies[2 * part + 1].start()
    c_t = jnp.transpose(c[...].reshape(POSITIONS, WIDTH))
    terms[:, :, 3] = dot(c_t, ctx[...]).astype(BF).reshape(ROWS, 2, 48, HALF_WIDTH)
    copies[6].start()
    copies[7].start()
    wait_all(extra + copies)


def row_kernel(
    core_ref, x_hbm, c_hbm, qkv_hbm, out_hbm, grads_hbm, ctx_hbm, keep_hbm, send_hbm,
    x, c, w_qkv, w_out, proj, gctx, grads, ctx, terms, sems, probs, dscores,
):
    copies = load(x_hbm, c_hbm, qkv_hbm, out_hbm, x, c, w_qkv, w_out, sems, 0)
    project(copies, x, c, w_qkv, w_out, proj, gctx)
    def products(pair, start):
        lanes = slice(pair * PAIR, (pair + 1) * PAIR)
        stop = start + BLOCK
        query, grad = proj[start:stop, lanes], gctx[start:stop, lanes]
        keys = [half_lanes(proj[:stop, HALF_WIDTH + pair * PAIR : HALF_WIDTH + (pair + 1) * PAIR], h) for h in range(2)]
        values = [
            half_lanes(proj[:stop, 2 * HALF_WIDTH + pair * PAIR : 2 * HALF_WIDTH + (pair + 1) * PAIR], h)
            for h in range(2)
        ]
        scores = [dot_nt(query, key) for key in keys]
        return pair, start, keys, values, scores, [dot_nt(grad, value) for value in values]

    def softmax(pair, start, keys, values, scores, grad_weights):
        lanes = slice(pair * PAIR, (pair + 1) * PAIR)
        stop = start + BLOCK
        outs, dqs = [], []
        weights = [probabilities(scores[half], start) for half in range(2)]
        for half in range(2):
            rounded = weights[half].astype(BF)
            probs[pair, half, start:stop, :stop] = rounded
            outs.append(dot(rounded, values[half]))
            delta = jnp.sum(weights[half] * grad_weights[half], axis=-1, keepdims=True)
            ds = (weights[half] * (grad_weights[half] - delta)).astype(BF)
            dscores[pair, half, start:stop, :stop] = ds
            dqs.append(dot(ds, keys[half]))
        ctx[start:stop, lanes] = (outs[0] + outs[1]).astype(BF)
        grads[start:stop, lanes] = ((dqs[0] + dqs[1]) * (HEAD_DIM ** -0.5)).astype(BF)

    def key_sums(pair):
        lanes = slice(pair * PAIR, (pair + 1) * PAIR)
        k_lanes = slice(HALF_WIDTH + pair * PAIR, HALF_WIDTH + (pair + 1) * PAIR)
        v_lanes = slice(2 * HALF_WIDTH + pair * PAIR, 2 * HALF_WIDTH + (pair + 1) * PAIR)
        query_t = jnp.transpose(proj[:, lanes])
        grad_t = jnp.transpose(gctx[:, lanes])
        for start in range(0, POSITIONS, BLOCK):
            stop = start + BLOCK
            for place, left, right in ((k_lanes, query_t, dscores), (v_lanes, grad_t, probs)):
                both = jnp.concatenate(
                    [
                        dot(left[half * HEAD_DIM : (half + 1) * HEAD_DIM, start:], right[pair, half, start:, start:stop])
                        for half in range(2)
                    ],
                    axis=0,
                )
                grads[start:stop, place] = jnp.transpose(both.astype(BF))

    order = [(pair, start) for pair in range(PAIRS) for start in range(0, POSITIONS, BLOCK)]
    held = products(*order[0])
    for index, (pair, start) in enumerate(order):
        following = products(*order[index + 1]) if index + 1 < len(order) else None
        softmax(*held)
        held = following
        if start and pair:
            key_sums(pair - 1)
    key_sums(PAIRS - 1)
    core = core_ref[0]
    targets = [(1 - core, send_hbm), (core, keep_hbm)]
    weight_terms(x, c, grads, ctx, terms, targets, sems, [(grads, grads_hbm), (ctx, ctx_hbm)])


def column_kernel(
    core_ref, both_hbm, qkv_hbm, out_hbm, after, back_hbm, keep_hbm, send_hbm,
    x, c, w_qkv, w_out, proj, gctx, grads, ctx, terms, sems, back,
):
    x_hbm, c_hbm = both_hbm.at[:, 0], both_hbm.at[:, 1]
    copies = load(x_hbm, c_hbm, qkv_hbm, out_hbm, x, c, w_qkv, w_out, sems, HALF_WIDTH)
    project(copies, x, c, w_qkv, w_out, proj, gctx)
    size = ROWS * CHUNK
    chunks = COLUMNS // CHUNK
    line = lax.broadcasted_iota(jnp.int32, (size, size), 0)
    across = lax.broadcasted_iota(jnp.int32, (size, size), 1)
    allowed = ((line % CHUNK) == (across % CHUNK)) & (across <= line)
    allowed = jnp.concatenate([allowed.astype(F32)] * chunks, axis=0) > 0

    def twice(array):
        return jnp.concatenate([half_lanes(array, 0), half_lanes(array, 1)], axis=0)

    def gather(ref, base):
        whole = ref[:, base : base + PAIR].reshape(ROWS, COLUMNS, PAIR)
        return [
            whole[:, t * CHUNK : (t + 1) * CHUNK].reshape(size, PAIR) for t in range(chunks)
        ]

    def scatter(ref, base, pieces):
        whole = jnp.concatenate([p.reshape(ROWS, CHUNK, PAIR) for p in pieces], axis=1)
        ref[:, base : base + PAIR] = whole.reshape(POSITIONS, PAIR)

    def products(pair):
        base = pair * PAIR
        query, key, value = [gather(proj, part * HALF_WIDTH + base) for part in range(3)]
        grad = gather(gctx, base)
        keys, values, queries, grad_parts = [[twice(t) for t in part] for part in (key, value, query, grad)]
        scores = jnp.concatenate([dot_nt(a, b) for a, b in zip(query, keys)], axis=0)
        grad_weights = jnp.concatenate([dot_nt(a, b) for a, b in zip(grad, values)], axis=0)
        return base, keys, values, queries, grad_parts, scores, grad_weights

    def finish(base, keys, values, queries, grad_parts, scores, grad_weights):
        rounded, dscores = [], []
        for half in range(2):
            lanes = slice(half * size, (half + 1) * size)
            weights = chunk_probabilities(scores[:, lanes], allowed)
            rounded.append(weights.astype(BF))
            part = grad_weights[:, lanes]
            delta = jnp.sum(weights * part, axis=-1, keepdims=True)
            dscores.append((weights * (part - delta)).astype(BF))
        outs, dqs, dks, dvs = [], [], [], []
        for t in range(chunks):
            rows = slice(t * size, (t + 1) * size)
            wide = [jnp.concatenate([pieces[0][rows], pieces[1][rows]], axis=1) for pieces in (rounded, dscores)]
            tall = [jnp.concatenate([pieces[0][rows], pieces[1][rows]], axis=0) for pieces in (rounded, dscores)]
            outs.append(dot(wide[0], values[t]).astype(BF))
            dqs.append((dot(wide[1], keys[t]) * (HEAD_DIM ** -0.5)).astype(BF))
            dks.append(dot_tn(tall[1], queries[t]).astype(BF))
            dvs.append(dot_tn(tall[0], grad_parts[t]).astype(BF))
        scatter(ctx, base, outs)
        scatter(grads, base, dqs)
        scatter(grads, HALF_WIDTH + base, dks)
        scatter(grads, 2 * HALF_WIDTH + base, dvs)

    for item in [products(pair) for pair in range(PAIRS)]:
        finish(*item)
    core = core_ref[0]
    targets = [(1 - core, send_hbm), (core, keep_hbm)]
    back[:, WIDTH:] = ctx[...]
    for start in range(0, WIDTH, BLOCK):
        columns = slice(start, start + BLOCK)
        back[:, columns] = dot_nt(grads[...], w_qkv[columns]).astype(BF)
    weight_terms(x, c, grads, ctx, terms, targets, sems, [(back, back_hbm)])


def wait_all(copies):
    for copy in copies:
        copy.wait()


def start_all(copies):
    for copy in copies:
        copy.start()
    return copies


def weight_copies(qkv_hbm, w_qkv, sems, first):
    return [
        pltpu.make_async_copy(
            qkv_hbm.at[:, pl.ds(part * WIDTH + first, HALF_WIDTH)], w_qkv.at[part], sems.at[part]
        )
        for part in range(3)
    ]


def grads_times_weights(grads, w_qkv, columns):
    return sum(
        dot_nt(grads[:, part * HALF_WIDTH : (part + 1) * HALF_WIDTH], w_qkv[part, columns]) for part in range(3)
    )


def final_kernel(
    grads_hbm, ctx_hbm, back_hbm, qkv_hbm, out_hbm, attention_hbm, normed_hbm,
    grads, ctx, back, w_qkv, w_out, attention, normed, sems, out_sems,
):
    ins = start_all(
        [
            pltpu.make_async_copy(source, target, sems.at[3 + index])
            for index, (source, target) in enumerate(
                ((ctx_hbm, ctx), (back_hbm, back), (out_hbm, w_out), (grads_hbm, grads))
            )
        ]
        + weight_copies(qkv_hbm, w_qkv, sems, 0)
    )
    outs = []
    wait_all(ins[:3])
    for index in range(3):
        columns = slice(index * BLOCK, (index + 1) * BLOCK)
        span = pl.ds(index * BLOCK, BLOCK)
        attention[:, columns] = (
            dot_nt(ctx[...], w_out[columns, :HALF_WIDTH]) + dot_nt(back[:, WIDTH:], w_out[columns, HALF_WIDTH:])
        ).astype(BF)
        outs += start_all(
            [pltpu.make_async_copy(attention.at[:, span], attention_hbm.at[:, span], out_sems.at[0, index])]
        )
    wait_all(ins[3:])
    for index in range(3):
        columns = slice(index * BLOCK, (index + 1) * BLOCK)
        span = pl.ds(index * BLOCK, BLOCK)
        normed[:, columns] = (
            back[:, columns].astype(F32) + grads_times_weights(grads, w_qkv, columns)
        ).astype(BF)
        outs += start_all([pltpu.make_async_copy(normed.at[:, span], normed_hbm.at[:, span], out_sems.at[1, index])])
    wait_all(outs)


def order_kernel(*refs):
    pass


def pack_kernel(x_hbm, c_hbm, both_hbm, both, sems, out_sems):
    spans = [pl.ds(2 * index, 2) for index in range(4)]
    ins = start_all(
        [
            pltpu.make_async_copy(source.at[span], both.at[span, place], sems.at[place, index])
            for index, span in enumerate(spans)
            for place, source in enumerate((x_hbm, c_hbm))
        ]
    )
    outs = []
    for index, span in enumerate(spans):
        wait_all(ins[2 * index : 2 * index + 2])
        outs += start_all([pltpu.make_async_copy(both.at[span], both_hbm.at[span], out_sems.at[index])])
    wait_all(outs)


def pair_sum_kernel(x_ref, keep_hbm, received_hbm, *refs):
    out_hbms = refs[-8:-4]
    terms, totals, sems, out_sems = refs[-4:]
    ins, outs = [], []
    order = (1, 3, 2, 0)
    for step in order:
        place = pl.ds(2 * lax.rem(x_ref[0] + step, 4), 2)
        for index, source in enumerate((keep_hbm, received_hbm)):
            ins += start_all(
                [pltpu.make_async_copy(source.at[place], terms.at[step, index], sems.at[index, step])]
            )
    for index, step in enumerate(order):
        wait_all(ins[2 * index : 2 * index + 2])
        totals[step] = (terms[step, 0].astype(F32) + terms[step, 1].astype(F32)).astype(BF)
        outs += start_all([pltpu.make_async_copy(totals.at[step], out_hbms[step], out_sems.at[step])])
    wait_all(outs)


def ring_sum_kernel(*refs):
    in_hbms, (out_hbm, terms, totals, sems, out_sems) = refs[:8], refs[9:]
    ins = [
        start_all(
            [
                pltpu.make_async_copy(source.at[z_hi], terms.at[index, z_hi], sems.at[index, z_hi])
                for index, source in enumerate(in_hbms)
            ]
        )
        for z_hi in range(2)
    ]
    outs = []
    for z_hi in range(2):
        wait_all(ins[z_hi])
        for half in range(2):
            total = sum(terms[4 * half + step, z_hi].astype(F32) for step in range(4))
            for z_lo in range(2):
                totals[z_hi, :, z_lo, half] = total[:, 24 * z_lo : 24 * z_lo + 24].astype(BF)
        outs += start_all([pltpu.make_async_copy(totals.at[z_hi], out_hbm.at[z_hi], out_sems.at[z_hi])])
    wait_all(outs)


def group_sum_kernel(pieces_hbm, after, out_hbm, pieces, total, sems, in_sems):
    ins = start_all(
        [
            pltpu.make_async_copy(pieces_hbm.at[pl.ds(4 * index, 4)], pieces.at[pl.ds(4 * index, 4)], in_sems.at[index])
            for index in range(4)
        ]
    )
    parts = []
    for index in range(4):
        ins[index].wait()
        parts.append(jnp.sum(pieces[4 * index : 4 * index + 4].astype(F32), axis=0))
    total[...] = sum(parts).astype(BF)
    wait_all(
        start_all([pltpu.make_async_copy(total, out_hbm.at[place], sems.at[place]) for place in range(8)])
    )


def assemble_kernel(factor, whole, qkv_hbm, out_hbm, qkv_grad, out_grad, sems):
    outs = []
    for z_lo in range(2):
        rows, span = slice(24 * z_lo, 24 * z_lo + 24), pl.ds(24 * z_lo, 24)
        for part in range(4):
            for half in range(2):
                value = whole[4 * z_lo + part, half].astype(F32) * factor
                start = half * HALF_WIDTH
                if part < 3:
                    start += part * WIDTH
                    qkv_grad[rows, start : start + HALF_WIDTH] = value
                else:
                    out_grad[rows, start : start + HALF_WIDTH] = value
        outs += start_all(
            [
                pltpu.make_async_copy(qkv_grad.at[span], qkv_hbm.at[span], sems.at[0, z_lo]),
                pltpu.make_async_copy(out_grad.at[span], out_hbm.at[span], sems.at[1, z_lo]),
            ]
        )
    wait_all(outs)


SMEM = pl.BlockSpec(memory_space=pltpu.SMEM)
HBM = pl.BlockSpec(memory_space=pltpu.HBM)


def buffer(*dims, dtype=BF):
    return pltpu.VMEM(dims, dtype)


def copy_sems(*dims):
    return pltpu.SemaphoreType.DMA(dims)


def shape(*dims, dtype=BF):
    return jax.ShapeDtypeStruct(dims, dtype)


def call(kernel, out_shape, flops, scratch, arrays, mib=64, held=None, aliases=None):
    scalars = sum(1 for array in arrays if array.ndim == 1)
    return pl.pallas_call(
        kernel,
        out_shape=out_shape,
        in_specs=[SMEM] * scalars + [held or HBM] * (len(arrays) - scalars),
        out_specs=jax.tree.map(lambda _: HBM, out_shape),
        scratch_shapes=scratch,
        input_output_aliases=aliases or {},
        compiler_params=pltpu.CompilerParams(vmem_limit_bytes=mib * MIB),
        cost_estimate=pl.CostEstimate(flops=flops, bytes_accessed=2 ** 16, transcendentals=0),
    )(*arrays)


def sublayer(kernel, dims, out_shapes, scratch, *arrays):
    return call(
        kernel,
        (*out_shapes, shape(ROWS, 4, 48, HALF_WIDTH), shape(ROWS, 4, 48, HALF_WIDTH)),
        2 * 10 ** 10,
        [
            buffer(*dims),
            buffer(*dims),
            buffer(WIDTH, 3 * HALF_WIDTH),
            buffer(WIDTH, HALF_WIDTH),
            buffer(POSITIONS, 3 * HALF_WIDTH),
            buffer(POSITIONS, HALF_WIDTH),
            buffer(POSITIONS, 3 * HALF_WIDTH),
            buffer(POSITIONS, HALF_WIDTH),
            buffer(ROWS, 2, 4, 48, HALF_WIDTH),
            copy_sems(10),
            *scratch,
        ],
        arrays,
        mib=64,
    )


def swap(part, axis, groups=None):
    return lax.all_to_all(part, axis, split_axis=0, concat_axis=0, tiled=True, axis_index_groups=groups)


def plane_groups():
    def flat(x, z_hi, core, z_lo, y):
        return ((x * 2 + z_hi) * 2 + core) * 8 + z_lo * 4 + y

    return [
        [flat(x, z_hi, core, z_lo, y) for z_hi in range(2) for y in range(4) for z_lo in range(2)]
        for x in range(4)
        for core in range(2)
    ]


def exchange(send):
    return lax.ppermute(send, "dp", [(i, i ^ 1) for i in range(16)])


def pair_sum(x_index, keep, send, *after):
    return call(
        pair_sum_kernel,
        (shape(2, 4, 48, HALF_WIDTH),) * 4,
        2 * 10 ** 9,
        [buffer(4, 2, 2, 4, 48, HALF_WIDTH), buffer(4, 2, 4, 48, HALF_WIDTH), copy_sems(2, 4), copy_sems(4)],
        (x_index, keep, exchange(send), *after),
    )


def ring(parts):
    return [parts[0]] + [
        lax.ppermute(parts[step], "dp", [(i, (i + 4 * step) % 16) for i in range(16)]) for step in (2, 3, 1)
    ]


def body(normed, cotangent, qkv_weight, out_weight):
    x, c = normed[0], cotangent[0]
    dp = lax.axis_index("dp")
    core = (dp % 2).reshape(1)
    x_index = (dp // 4).reshape(1)
    grid_dims = (ROWS, COLUMNS, WIDTH)
    both = call(
        pack_kernel,
        shape(ROWS, 2, COLUMNS, WIDTH),
        10 ** 6,
        [buffer(ROWS, 2, COLUMNS, WIDTH), copy_sems(2, 4), copy_sems(4)],
        (x.reshape(grid_dims), c.reshape(grid_dims)),
    )
    both = swap(both, "ctx")
    grads_row, ctx_row, keep_row, send_row = sublayer(
        row_kernel,
        (POSITIONS, WIDTH),
        [shape(POSITIONS, 3 * HALF_WIDTH), shape(POSITIONS, HALF_WIDTH)],
        [buffer(PAIRS, 2, POSITIONS, POSITIONS)] * 2,
        core, x, c, qkv_weight, out_weight,
    )
    terms_row = ring(pair_sum(x_index, keep_row, send_row))
    back_width = WIDTH + HALF_WIDTH
    back, keep_col, send_col = sublayer(
        column_kernel,
        grid_dims,
        [shape(POSITIONS, back_width)],
        [buffer(POSITIONS, back_width)],
        core, both, qkv_weight, out_weight, terms_row[0],
    )
    terms_row[1] = order = call(
        order_kernel, shape(2, 4, 48, HALF_WIDTH), 4 * 10 ** 10, [], (back, *terms_row[1:]), aliases={1: 0}
    )
    parts = pair_sum(x_index, keep_col, send_col, order)
    terms_col = ring(parts)
    back = swap(back.reshape(ROWS, COLUMNS, back_width), "ctx").reshape(POSITIONS, back_width)
    attention_out, normed_grad = call(
        final_kernel,
        (shape(POSITIONS, WIDTH),) * 2,
        4 * 10 ** 9,
        [
            buffer(POSITIONS, 3 * HALF_WIDTH),
            buffer(POSITIONS, HALF_WIDTH),
            buffer(POSITIONS, back_width),
            buffer(3, WIDTH, HALF_WIDTH),
            buffer(WIDTH, WIDTH),
            buffer(POSITIONS, WIDTH),
            buffer(POSITIONS, WIDTH),
            copy_sems(7),
            copy_sems(2, 4),
        ],
        (grads_row, ctx_row, back, qkv_weight, out_weight),
        mib=64,
    )
    terms = call(
        ring_sum_kernel,
        shape(2, 4, 2, 2, 24, HALF_WIDTH),
        2 * 10 ** 9,
        [buffer(8, 2, 4, 48, HALF_WIDTH), buffer(2, 4, 2, 2, 24, HALF_WIDTH), copy_sems(8, 2), copy_sems(2)],
        (*terms_row, *terms_col, back),
    )
    pieces = swap(terms.reshape(16, 2, 24, HALF_WIDTH), ("dp", "ctx"), plane_groups())
    own = call(
        group_sum_kernel,
        shape(8, 2, 24, HALF_WIDTH),
        10 ** 9,
        [buffer(16, 2, 24, HALF_WIDTH), buffer(2, 24, HALF_WIDTH), copy_sems(8), copy_sems(4)],
        (pieces, attention_out),
    )
    whole = swap(own, "ctx")
    factor = (lax.axis_size("dp") * lax.axis_size("ctx") * POSITIONS) ** (-0.5)
    qkv_grad, out_grad = call(
        functools.partial(assemble_kernel, factor),
        (shape(48, 3 * WIDTH, dtype=F32), shape(48, WIDTH, dtype=F32)),
        10 ** 6,
        [
            buffer(48, 3 * WIDTH, dtype=F32),
            buffer(48, WIDTH, dtype=F32),
            copy_sems(2, 2),
        ],
        (whole,),
        mib=8,
        held=pl.BlockSpec(memory_space=pltpu.VMEM),
    )
    return (attention_out[None], normed_grad[None], qkv_grad, out_grad)


def solution(mesh):
    placed = (P("dp", "ctx", None), P("dp", "ctx", None), P(), P())
    return jax.shard_map(
        body,
        mesh=mesh,
        in_specs=placed,
        out_specs=(P("dp", "ctx", None), P("dp", "ctx", None), P("dp", None), P("dp", None)),
        check_vma=False,
    )
```
